32 devices in a mesh: ctx: 8 (over y, x, core), fsdp: 4 (over z).
Axes of the slice: x: 2, y: 2, z: 4, core: 2. Of those that a mesh axis runs over, the one named last changes fastest.
Arguments:
- tokens: bfloat16 [4, 1024, 1536], P('fsdp', 'ctx'), may hold values from -6 to 6
- cotangent: bfloat16 [4, 1024, 1536], P('fsdp', 'ctx'), may hold values from -6 to 6
- block_position: int32 [16], replicated, may hold values from 0 to 15, as said below
- w_query: bfloat16 [1536, 1536], P(('ctx', 'fsdp')), may hold values from -0.15625 to 0.15625
- key_weight: bfloat16 [1536, 256], P(('ctx', 'fsdp')), may hold values from -0.15625 to 0.15625
- value_weight: bfloat16 [1536, 256], P(('ctx', 'fsdp')), may hold values from -0.15625 to 0.15625
- w_output: bfloat16 [1536, 1536], P(('ctx', 'fsdp')), may hold values from -2.5 to 2.5
- w_gate: bfloat16 [8960, 1536], P(('ctx', 'fsdp')), may hold values from -0.15625 to 0.15625
- w_up: bfloat16 [8960, 1536], P(('ctx', 'fsdp')), may hold values from -0.15625 to 0.15625
- w_down: bfloat16 [8960, 1536], P(('ctx', 'fsdp')), may hold values from -0.0625 to 0.0625
- projection_bias: bfloat16 [2048], replicated, may hold values from -3 to 3
- norm_gains: bfloat16 [2, 1536], replicated, may hold values from 0.5 to 1.5
- momentum_query: float32 [1536, 1536], P(('ctx', 'fsdp')), may hold values from -112 to 112
- key_momentum: float32 [1536, 256], P(('ctx', 'fsdp')), may hold values from -112 to 112
- value_momentum: float32 [1536, 256], P(('ctx', 'fsdp')), may hold values from -112 to 112
- momentum_output: float32 [1536, 1536], P(('ctx', 'fsdp')), may hold values from -112 to 112
- momentum_gate: float32 [8960, 1536], P(('ctx', 'fsdp')), may hold values from -112 to 112
- momentum_up: float32 [8960, 1536], P(('ctx', 'fsdp')), may hold values from -112 to 112
- momentum_down: float32 [8960, 1536], P(('ctx', 'fsdp')), may hold values from -112 to 112
- bias_momentum: float32 [2048], replicated, may hold values from -112 to 112
- momentum_gains: float32 [2, 1536], replicated, may hold values from -112 to 112
Outputs:
- out_tokens: bfloat16 [4, 1024, 1536], P('fsdp', 'ctx')
- grad_tokens: float32 [4, 1024, 1536], P('fsdp', 'ctx')
- grad_query: float32 [1536, 1536], P(('ctx', 'fsdp'))
- grad_key: float32 [1536, 256], P(('ctx', 'fsdp'))
- grad_value: float32 [1536, 256], P(('ctx', 'fsdp'))
- grad_output: float32 [1536, 1536], P(('ctx', 'fsdp'))
- grad_gate: float32 [8960, 1536], P(('ctx', 'fsdp'))
- grad_up: float32 [8960, 1536], P(('ctx', 'fsdp'))
- grad_down: float32 [8960, 1536], P(('ctx', 'fsdp'))
- moment_query: float32 [1536, 1536], P(('ctx', 'fsdp'))
- moment_key: float32 [1536, 256], P(('ctx', 'fsdp'))
- moment_value: float32 [1536, 256], P(('ctx', 'fsdp'))
- moment_output: float32 [1536, 1536], P(('ctx', 'fsdp'))
- moment_gate: float32 [8960, 1536], P(('ctx', 'fsdp'))
- moment_up: float32 [8960, 1536], P(('ctx', 'fsdp'))
- moment_down: float32 [8960, 1536], P(('ctx', 'fsdp'))
- update_query: float32 [1536, 1536], P(('ctx', 'fsdp'))
- update_key: float32 [1536, 256], P(('ctx', 'fsdp'))
- update_value: float32 [1536, 256], P(('ctx', 'fsdp'))
- update_output: float32 [1536, 1536], P(('ctx', 'fsdp'))
- update_gate: float32 [8960, 1536], P(('ctx', 'fsdp'))
- update_up: float32 [8960, 1536], P(('ctx', 'fsdp'))
- update_down: float32 [8960, 1536], P(('ctx', 'fsdp'))
- grad_bias: float32 [2048], replicated
- moment_bias: float32 [2048], replicated
- update_bias: float32 [2048], replicated
- grad_gains: float32 [2, 1536], replicated
- moment_gains: float32 [2, 1536], replicated
- update_gains: float32 [2, 1536], replicated
The draws below stay inside these ranges and needn't reach their ends.
Inputs may be any that keep to these rules, and one draw needn't show every extreme that they name: `block_position`: A permutation of the blocks 0 to 15; entries 2 c and 2 c + 1, the two blocks of ctx index c, sum to 15.
All inputs are finite; a program needn't handle non-finite values.
Results may differ from the reference program's by a relative error of at most 0.02.
Values may be sent and summed in bfloat16 or wider, within the bound.
No kernel may reach another device: no remote copies, remote signals or barrier semaphores. Data moves between devices by JAX's collectives and lax.ppermute only.
A program may use at most 320 MiB of HBM per device.

```python
import math
import jax
import jax.numpy as jnp
from jax import lax

MODEL_DIM = 1536
QUERY_HEADS = 12
KEY_VALUE_HEADS = 2
HEAD_DIM = 128
FF = 8960
TOKENS_PER_SHARD = 128
NS_ITERS = 2
BLK = 64
SEQUENCE_TOKENS = 1024
BLOCKS = 16
SEQS = 4
N_CTX = 8
N_FSDP = 4


def draw_block_position(key, part):
    half_count = BLOCKS // 2
    order = jax.random.permutation(jax.random.fold_in(key, 11), half_count)
    flipped = jax.random.randint(jax.random.fold_in(key, 12), (half_count,), 0, 2)
    lower_block = order
    upper_block = BLOCKS - 1 - order
    leading = jnp.where(flipped == 1, upper_block, lower_block)
    trailing = jnp.where(flipped == 1, lower_block, upper_block)
    return jnp.stack([leading, trailing], axis=1).reshape(BLOCKS).astype(jnp.int32)


def shard_levels(stream_key, dims, cuts, least, high):
    level, own = 1.0, jax.random.fold_in(stream_key, 6)
    for position, parts in cuts:
        steps = jnp.exp(jax.random.uniform(jax.random.fold_in(own, position), (parts,), jnp.float32, least / len(cuts), high / len(cuts)))
        level = level * jnp.repeat(steps, dims[position] // parts).reshape([-1 if axis == position else 1 for axis in range(len(dims))])
    return level


def normal_values(own_key, extent, spread, bound, shards=(), kind=jnp.bfloat16):
    level = shard_levels(own_key, extent, shards, -0.22, 0.18) if shards else 1.0
    entries = jax.random.normal(own_key, extent, jnp.float32) * spread * level
    return jnp.minimum(jnp.maximum(entries, -bound), bound).astype(kind)


def setup_inputs(seed: int = 0) -> dict:
    seeds = jax.random.split(jax.random.key(seed), 22)
    tokens = normal_values(seeds[0], (SEQS, SEQUENCE_TOKENS, MODEL_DIM), 1.0, 6.0, ((0, 4), (1, 8)))
    cotangent = normal_values(seeds[1], (SEQS, SEQUENCE_TOKENS, MODEL_DIM), 1.0, 6.0, ((0, 4), (1, 8)))
    block_position = draw_block_position(jax.random.fold_in(seeds[21], 71), 0)
    w_query = normal_values(seeds[3], (MODEL_DIM, QUERY_HEADS * HEAD_DIM), MODEL_DIM ** -0.5, 0.15625, ((0, 32),))
    key_weight = normal_values(seeds[4], (MODEL_DIM, KEY_VALUE_HEADS * HEAD_DIM), MODEL_DIM ** -0.5, 0.15625, ((0, 32),))
    value_weight = normal_values(seeds[5], (MODEL_DIM, KEY_VALUE_HEADS * HEAD_DIM), MODEL_DIM ** -0.5, 0.15625, ((0, 32),))
    w_output = normal_values(seeds[6], (QUERY_HEADS * HEAD_DIM, MODEL_DIM), (max(MODEL_DIM // 256, 4)) ** -0.5, 2.5, ((0, 32),))
    w_gate = normal_values(seeds[7], (FF, MODEL_DIM), MODEL_DIM ** -0.5, 0.15625, ((0, 32),))
    w_up = normal_values(seeds[8], (FF, MODEL_DIM), MODEL_DIM ** -0.5, 0.15625, ((0, 32),))
    w_down = normal_values(seeds[9], (FF, MODEL_DIM), FF ** -0.5, 0.0625, ((0, 32),))
    projection_bias = normal_values(seeds[10], (QUERY_HEADS * HEAD_DIM + 2 * KEY_VALUE_HEADS * HEAD_DIM,), 0.5, 3.0)
    norm_gains = jnp.clip(1.0 + 0.1 * jax.random.normal(seeds[11], (2, MODEL_DIM), jnp.float32), 0.5, 1.5).astype(jnp.bfloat16)
    momentum_query = normal_values(seeds[12], (MODEL_DIM, QUERY_HEADS * HEAD_DIM), (0.3 * (TOKENS_PER_SHARD * N_CTX * N_FSDP) ** 0.5), 112.0, ((0, 32),), jnp.float32)
    key_momentum = normal_values(seeds[13], (MODEL_DIM, KEY_VALUE_HEADS * HEAD_DIM), (0.3 * (TOKENS_PER_SHARD * N_CTX * N_FSDP) ** 0.5), 112.0, ((0, 32),), jnp.float32)
    value_momentum = normal_values(seeds[14], (MODEL_DIM, KEY_VALUE_HEADS * HEAD_DIM), (0.3 * (TOKENS_PER_SHARD * N_CTX * N_FSDP) ** 0.5), 112.0, ((0, 32),), jnp.float32)
    momentum_output = normal_values(seeds[15], (QUERY_HEADS * HEAD_DIM, MODEL_DIM), (0.3 * (TOKENS_PER_SHARD * N_CTX * N_FSDP) ** 0.5), 112.0, ((0, 32),), jnp.float32)
    momentum_gate = normal_values(seeds[16], (FF, MODEL_DIM), (0.3 * (TOKENS_PER_SHARD * N_CTX * N_FSDP) ** 0.5), 112.0, ((0, 32),), jnp.float32)
    momentum_up = normal_values(seeds[17], (FF, MODEL_DIM), (0.3 * (TOKENS_PER_SHARD * N_CTX * N_FSDP) ** 0.5), 112.0, ((0, 32),), jnp.float32)
    momentum_down = normal_values(seeds[18], (FF, MODEL_DIM), (0.3 * (TOKENS_PER_SHARD * N_CTX * N_FSDP) ** 0.5), 112.0, ((0, 32),), jnp.float32)
    bias_momentum = normal_values(seeds[19], (QUERY_HEADS * HEAD_DIM + 2 * KEY_VALUE_HEADS * HEAD_DIM,), (0.3 * (TOKENS_PER_SHARD * N_CTX * N_FSDP) ** 0.5), 112.0, (), jnp.float32)
    momentum_gains = normal_values(seeds[20], (2, MODEL_DIM), (0.3 * (TOKENS_PER_SHARD * N_CTX * N_FSDP) ** 0.5), 112.0, (), jnp.float32)
    return {"tokens": tokens, "cotangent": cotangent, "block_position": block_position, "w_query": w_query, "key_weight": key_weight, "value_weight": value_weight, "w_output": w_output, "w_gate": w_gate, "w_up": w_up, "w_down": w_down, "projection_bias": projection_bias, "norm_gains": norm_gains, "momentum_query": momentum_query, "key_momentum": key_momentum, "value_momentum": value_momentum, "momentum_output": momentum_output, "momentum_gate": momentum_gate, "momentum_up": momentum_up, "momentum_down": momentum_down, "bias_momentum": bias_momentum, "momentum_gains": momentum_gains}


NORM_EPSILON = 1e-06
ROPE_BASE = 1000000.0
POLY_ONE = 3.4445
POLY_THREE = -4.775
POLY_FIVE = 2.0315
MOMENTUM = 0.95
STEP_SCALE = 0.06
VECTOR_STEP = 0.1
MASK_FILL = -1e+30
HIGHEST = lax.Precision.HIGHEST

@jax.custom_vjp
def lowered_precision(v):
    return lax.optimization_barrier(v.astype(jnp.bfloat16)).astype(jnp.float32)

@jax.custom_vjp
def low_back(v):
    return v

def low_keep(v):
    return (lowered_precision(v), None)

def low_pass(kept, grad):
    return (grad,)

def back_keep(v):
    return (v, None)

def back_low(kept, grad):
    return (lowered_precision(grad),)
lowered_precision.defvjp(low_keep, low_pass)
low_back.defvjp(back_keep, back_low)

def matmul(left, right):
    return jnp.dot(left, right, precision=HIGHEST, preferred_element_type=jnp.float32)

def matmul_nt(left, right):
    return lax.dot_general(left, right, (((1,), (1,)), ((), ())), precision=HIGHEST, preferred_element_type=jnp.float32)

def rope_tables(positions, head_size):
    half_width = head_size // 2
    ratios = jnp.arange(half_width, dtype=jnp.float32) * (2.0 / head_size)
    frequency = jnp.exp(-math.log(ROPE_BASE) * ratios)
    angles = positions.astype(jnp.float32)[:, None] * frequency[None, :]
    return (jnp.cos(angles), jnp.sin(angles))

def apply_rotary(values, cosine_lookup, sine_lookup):
    half_width = values.shape[-1] // 2
    front_half = values[..., :half_width]
    back_half = values[..., half_width:]
    cosine_rows = cosine_lookup[:, None, :]
    sine_rows = sine_lookup[:, None, :]
    return jnp.concatenate([front_half * cosine_rows - back_half * sine_rows, back_half * cosine_rows + front_half * sine_rows], axis=-1)

def norm_apply(values, gain):
    scale_rows = lax.rsqrt(lax.optimization_barrier(jnp.mean(values * values, axis=-1, keepdims=True)) + NORM_EPSILON)
    return values * scale_rows * gain

def attend(rotated_queries, rotated_keys, value_lowered, positions):
    heads_per_group = QUERY_HEADS // KEY_VALUE_HEADS
    block_row_slice = math.gcd(SEQUENCE_TOKENS, 512)
    block_count = SEQUENCE_TOKENS // block_row_slice
    score_scale = 1.0 / math.sqrt(HEAD_DIM)
    key_head_rows = rotated_keys.reshape(SEQUENCE_TOKENS, KEY_VALUE_HEADS, HEAD_DIM)
    value_head_rows = value_lowered.reshape(SEQUENCE_TOKENS, KEY_VALUE_HEADS, HEAD_DIM)

    def one_block(inputs):
        query_rows, query_positions = inputs
        grouped_queries = query_rows.reshape(block_row_slice, KEY_VALUE_HEADS, heads_per_group, HEAD_DIM)
        scores = low_back(jnp.einsum('qkgd,skd->kgqs', grouped_queries, key_head_rows, precision=HIGHEST) * score_scale)
        visible = positions[None, :] <= query_positions[:, None]
        scores = jnp.where(visible[None, None], scores, MASK_FILL)
        weights = jax.nn.softmax(scores, axis=-1)
        combined_heads = jnp.einsum('kgqs,skd->qkgd', lowered_precision(weights), value_head_rows, precision=HIGHEST)
        return combined_heads.reshape(block_row_slice, QUERY_HEADS * HEAD_DIM)
    outputs = lax.map(jax.checkpoint(one_block), (rotated_queries.reshape(block_count, block_row_slice, QUERY_HEADS, HEAD_DIM), positions.reshape(block_count, block_row_slice)))
    return outputs.reshape(SEQUENCE_TOKENS, QUERY_HEADS * HEAD_DIM)

def forward(layer_input, w_query, key_weight, value_weight, w_output, w_gate, w_up, w_down, projection_bias, norm_gains, positions, cosine_lookup, sine_lookup):
    query_width = QUERY_HEADS * HEAD_DIM
    key_value_width = KEY_VALUE_HEADS * HEAD_DIM
    normed_one = lowered_precision(norm_apply(layer_input, norm_gains[0]))
    query_proj = low_back(matmul(normed_one, w_query) + projection_bias[:query_width])
    key_projected = low_back(matmul(normed_one, key_weight) + projection_bias[query_width:query_width + key_value_width])
    value_lowered = lowered_precision(low_back(matmul(normed_one, value_weight) + projection_bias[query_width + key_value_width:]))
    rotated_queries = lowered_precision(apply_rotary(query_proj.reshape(SEQUENCE_TOKENS, QUERY_HEADS, HEAD_DIM), cosine_lookup, sine_lookup))
    rotated_keys = lowered_precision(apply_rotary(key_projected.reshape(SEQUENCE_TOKENS, KEY_VALUE_HEADS, HEAD_DIM), cosine_lookup, sine_lookup))
    attended = lowered_precision(low_back(attend(rotated_queries, rotated_keys, value_lowered, positions)))
    hidden_one = layer_input + low_back(matmul(attended, w_output))
    normed_two = lowered_precision(norm_apply(hidden_one, norm_gains[1]))
    gate_values = low_back(matmul_nt(normed_two, w_gate))
    up_values = low_back(matmul_nt(normed_two, w_up))
    hidden = lowered_precision(jax.nn.silu(gate_values) * up_values)
    return hidden_one + low_back(matmul(hidden, w_down))

def orthogonalize(moment):
    current = lowered_precision(moment)
    factor = 1.0 / (jnp.sqrt(jnp.sum(current * current)) + 1e-07)
    for iteration in range(NS_ITERS):
        gram_matrix = matmul(current.T, current) * (factor * factor)
        gram_low = lowered_precision(gram_matrix)
        polynomial = lowered_precision(POLY_THREE * gram_matrix + POLY_FIVE * matmul(gram_low, gram_low))
        current = lowered_precision(factor * (POLY_ONE * current + matmul(current, polynomial)))
        factor = 1.0
    return current

def vector_step(old_state, gradient):
    fresh_state = MOMENTUM * old_state + gradient
    inverse_rms = lax.rsqrt(lax.optimization_barrier(jnp.mean(fresh_state * fresh_state, axis=-1, keepdims=True)) + NORM_EPSILON)
    return (fresh_state, -VECTOR_STEP * fresh_state * inverse_rms)

def reference(tokens, cotangent, block_position, w_query, key_weight, value_weight, w_output, w_gate, w_up, w_down, projection_bias, norm_gains, momentum_query, key_momentum, value_momentum, momentum_output, momentum_gate, momentum_up, momentum_down, bias_momentum, momentum_gains):
    positions = (block_position[:, None] * BLK + jnp.arange(BLK, dtype=jnp.int32)[None, :]).reshape(SEQUENCE_TOKENS).astype(jnp.int32)
    cosine_lookup, sine_lookup = rope_tables(positions, HEAD_DIM)
    params = tuple((weight_arg.astype(jnp.float32) for weight_arg in (w_query, key_weight, value_weight, w_output, w_gate, w_up, w_down, projection_bias, norm_gains)))

    def per_sequence(totals, inputs):
        seq_tokens, seq_cotangent = inputs

        def layer_apply(layer_input, *layer_params):
            return forward(layer_input, *layer_params, positions, cosine_lookup, sine_lookup)
        result, pullback = jax.vjp(layer_apply, seq_tokens.astype(jnp.float32), *params)
        gradients = pullback(seq_cotangent.astype(jnp.float32))
        totals = tuple((total_one + grad_one for total_one, grad_one in zip(totals, gradients[1:])))
        return (totals, (result.astype(jnp.bfloat16), gradients[0]))
    zeros_init = tuple((jnp.zeros(weight_arg.shape, jnp.float32) for weight_arg in params))
    totals, (out_tokens, grad_tokens) = lax.scan(per_sequence, zeros_init, (tokens, cotangent))
    moments = []
    updates = []
    states = (momentum_query, key_momentum, value_momentum, momentum_output, momentum_gate, momentum_up, momentum_down)
    for gradient, old_state in zip(totals[:7], states):
        fresh_state = MOMENTUM * old_state + gradient
        moments.append(fresh_state)
        row_total, col_total = fresh_state.shape
        updates.append(-STEP_SCALE * math.sqrt(max(row_total, col_total)) * orthogonalize(fresh_state))
    moment_bias, update_bias = vector_step(bias_momentum, totals[7])
    moment_gains, update_gains = vector_step(momentum_gains, totals[8])
    return (out_tokens, grad_tokens, totals[0], totals[1], totals[2], totals[3], totals[4], totals[5], totals[6], moments[0], moments[1], moments[2], moments[3], moments[4], moments[5], moments[6], updates[0], updates[1], updates[2], updates[3], updates[4], updates[5], updates[6], totals[7], moment_bias, update_bias, totals[8], moment_gains, update_gains)
```

```python
import math

import jax
import jax.numpy as jnp
import numpy as np
from jax import lax
from jax.sharding import PartitionSpec as P

QUERY_HEADS = 12
KEY_VALUE_HEADS = 2
HEAD_DIM = 128
CORES = 2

NORM_EPSILON = 1e-06
ROPE_BASE = 1000000.0
POLY_ONE = 3.4445
POLY_THREE = -4.775
POLY_FIVE = 2.0315
MOMENTUM = 0.95
STEP_SCALE = 0.06
VECTOR_STEP = 0.1
MASK_FILL = -1e30

F32 = jnp.float32
BF16 = jnp.bfloat16


def matmul(left, right):
    return jnp.dot(left, right, preferred_element_type=F32)


def matmul_nt(left, right):
    return lax.dot_general(left, right, (((1,), (1,)), ((), ())), preferred_element_type=F32)


def matmul_tn(left, right):
    return lax.dot_general(left, right, (((0,), (0,)), ((), ())), preferred_element_type=F32)


def after(value, *others):
    return lax.optimization_barrier((value,) + others)[0]


class Grid:
    def __init__(self, ctx_count, z_count):
        plane = ctx_count // CORES
        x_count = math.isqrt(plane)
        while plane % x_count:
            x_count -= 1
        self.x_count, self.y_count, self.z_count = x_count, plane // x_count, z_count

    def place(self):
        ctx = lax.axis_index("ctx")
        return (
            ctx // (CORES * self.x_count),
            (ctx // CORES) % self.x_count,
            ctx % CORES,
            lax.axis_index("fsdp"),
        )

    def shift(self, value, dy=0, dx=0, dc=0, dz=0, keep=None):
        y_count, x_count, z_count = self.y_count, self.x_count, self.z_count
        dy, dx, dc, dz = dy % y_count, dx % x_count, dc % CORES, dz % z_count
        if not (dy or dx or dc):
            if not dz:
                return value
            return lax.ppermute(value, "fsdp", [(z, (z + dz) % z_count) for z in range(z_count)])
        pairs = []
        for y in range(y_count):
            for x in range(x_count):
                for c in range(CORES):
                    to_y, to_x, to_c = (y + dy) % y_count, (x + dx) % x_count, (c + dc) % CORES
                    if keep is None or keep(to_y, to_x):
                        pairs.append(
                            ((y * x_count + x) * CORES + c, (to_y * x_count + to_x) * CORES + to_c)
                        )
        assert not dz
        return lax.ppermute(value, "ctx", pairs)

    def plane_gather(self, block):
        half = block.shape[0] // 2
        first, second = block[:half], block[half:]
        first = jnp.concatenate(
            [first] + [self.shift(first, dx=j) for j in range(1, self.x_count)]
        )
        second = jnp.concatenate(
            [second] + [self.shift(second, dy=j) for j in range(1, self.y_count)]
        )
        return jnp.concatenate(
            [first]
            + [self.shift(first, dy=j) for j in range(1, self.y_count)]
            + [second]
            + [self.shift(second, dx=j) for j in range(1, self.x_count)]
        )

    def plane_order(self, rows):
        half = rows // 2
        jy, jx, row = [], [], []
        for y in range(self.y_count):
            for x in range(self.x_count):
                for r in range(half):
                    jy.append(y), jx.append(x), row.append(r)
        for x in range(self.x_count):
            for y in range(self.y_count):
                for r in range(half, rows):
                    jy.append(y), jx.append(x), row.append(r)
        return np.array(jy), np.array(jx), np.array(row)

    def gather(self, block):
        slots = [block]
        for _ in range(1, self.z_count):
            slots.append(self.shift(slots[-1], dz=1))
        return [self.plane_gather(slot) for slot in slots]

    def plane_reduce(self, part):
        def step(rows, count, axis):
            size = rows.shape[0] // count
            total = rows[:size].astype(F32)
            for j in range(1, count):
                piece = rows[j * size : (j + 1) * size].astype(BF16)
                total = total + self.shift(piece, **{axis: -j}).astype(F32)
            return total

        half = part.shape[0] // 2
        first = step(step(part[:half], self.y_count, "dy"), self.x_count, "dx")
        second = step(step(part[half:], self.x_count, "dx"), self.y_count, "dy")
        return jnp.concatenate([first, second])

    def z_sum(self, parts):
        total = parts[0].astype(F32)
        for j in range(1, self.z_count):
            total = total + self.shift(parts[j].astype(BF16), dz=-j).astype(F32)
        return total

    def reduce(self, parts):
        return self.z_sum([self.plane_reduce(part) for part in parts])


def rope_tables(positions, head_size):
    half_width = head_size // 2
    ratios = jnp.arange(half_width, dtype=F32) * (2.0 / head_size)
    frequency = jnp.exp(-math.log(ROPE_BASE) * ratios)
    angles = positions.astype(F32)[:, None] * frequency[None, :]
    return (jnp.cos(angles), jnp.sin(angles))


def apply_rotary(values, cosine_lookup, sine_lookup):
    half_width = values.shape[-1] // 2
    front_half = values[..., :half_width]
    back_half = values[..., half_width:]
    cosine_rows = cosine_lookup[:, None, :]
    sine_rows = sine_lookup[:, None, :]
    return jnp.concatenate(
        [
            front_half * cosine_rows - back_half * sine_rows,
            back_half * cosine_rows + front_half * sine_rows,
        ],
        axis=-1,
    )


def norm_scale(values):
    return lax.rsqrt(jnp.mean(values * values, axis=-1, keepdims=True) + NORM_EPSILON)


def norm_back(values, scale_rows, gain, grad_normed):
    weighted = grad_normed * gain
    inner_mean = jnp.mean(weighted * values, axis=-1, keepdims=True)
    grad_values = (
        scale_rows * weighted - values * (scale_rows * scale_rows * scale_rows) * inner_mean
    )
    grad_gain = jnp.sum(grad_normed * values * scale_rows, axis=0)
    return (grad_values, grad_gain)


def vector_step(old_state, gradient):
    fresh_state = MOMENTUM * old_state + gradient
    inverse_rms = lax.rsqrt(
        jnp.mean(fresh_state * fresh_state, axis=-1, keepdims=True) + NORM_EPSILON
    )
    return (fresh_state, -VECTOR_STEP * fresh_state * inverse_rms)


def polynomials(gram):
    factor = 1.0 / (jnp.sqrt(jnp.trace(gram)) + 1e-07)
    gram_one = gram * (factor * factor)
    low_one = gram_one.astype(BF16)
    poly_one = (POLY_THREE * gram_one + POLY_FIVE * matmul(low_one, low_one)).astype(BF16)
    mixed = matmul(low_one, poly_one)
    gram_two = (
        (POLY_ONE * POLY_ONE) * gram_one
        + (2.0 * POLY_ONE) * mixed
        + matmul(poly_one, mixed.astype(BF16))
    )
    low_two = gram_two.astype(BF16)
    poly_two = (POLY_THREE * gram_two + POLY_FIVE * matmul(low_two, low_two)).astype(BF16)
    return factor, poly_one, poly_two


def advance(start, factor, poly_one, poly_two):
    middle = (factor * (POLY_ONE * start.astype(F32) + matmul(start, poly_one))).astype(BF16)
    return (POLY_ONE * middle.astype(F32) + matmul(middle, poly_two)).astype(BF16)


def shards(
    tokens,
    cotangent,
    block_position,
    w_query,
    key_weight,
    value_weight,
    w_output,
    w_gate,
    w_up,
    w_down,
    projection_bias,
    norm_gains,
    momentum_query,
    key_momentum,
    value_momentum,
    momentum_output,
    momentum_gate,
    momentum_up,
    momentum_down,
    bias_momentum,
    momentum_gains,
):
    shard_rows = tokens.shape[1]
    width = tokens.shape[2]
    ctx_count = lax.axis_size("ctx")
    z_count = lax.axis_size("fsdp")
    grid = Grid(ctx_count, z_count)
    y_count, x_count = grid.y_count, grid.x_count
    plane = y_count * x_count
    place_y, place_x, place_c, place_z = grid.place()
    ctx_rank = lax.axis_index("ctx")
    all_count = ctx_count * z_count
    half_block = shard_rows // 2
    query_width = QUERY_HEADS * HEAD_DIM
    key_value_width = KEY_VALUE_HEADS * HEAD_DIM
    heads_per_group = QUERY_HEADS // KEY_VALUE_HEADS
    grouped_rows = heads_per_group * shard_rows
    score_scale = 1.0 / math.sqrt(HEAD_DIM)
    weight_rows = w_query.shape[0]
    ff_rows = w_gate.shape[0]

    weight_block = jnp.concatenate([w_query, key_weight, value_weight, w_output], axis=1)
    weight_chunks = grid.gather(weight_block)
    weight_parts = []
    for chunk in weight_chunks:
        weight_parts += [chunk, grid.shift(chunk, dc=1)]
    full_weights = jnp.concatenate(weight_parts)
    qkv_width = query_width + 2 * key_value_width
    full_qkv = full_weights[:, :qkv_width]
    full_output = full_weights[:, qkv_width:]
    jy, jx, row = grid.plane_order(weight_rows)
    source_y = (place_y - jnp.asarray(jy)) % y_count
    source_x = (place_x - jnp.asarray(jx)) % x_count
    pieces = []
    for jz in range(z_count):
        for jc in range(CORES):
            device = ((source_y * x_count + source_x) * CORES + (place_c - jc) % CORES) * z_count
            pieces.append((device + (place_z - jz) % z_count) * weight_rows + jnp.asarray(row))
    relative_rows = jnp.concatenate(pieces)
    reorder = (jnp.arange(width, dtype=jnp.int32)[:, None] == relative_rows[None, :]).astype(BF16)

    inputs = tokens[0].astype(F32)
    grad_mid = cotangent[0]
    grad_out = grad_mid.astype(F32)
    gain_one = norm_gains[0].astype(F32)
    gain_two = norm_gains[1].astype(F32)
    bias_values = projection_bias.astype(F32)

    ff_block = jnp.concatenate([w_gate, w_up, w_down])
    ff_other = grid.shift(ff_block, dc=1)
    gate_pair = jnp.concatenate([w_gate, ff_other[:ff_rows]])
    up_pair = jnp.concatenate([w_up, ff_other[ff_rows : 2 * ff_rows]])
    down_pair = jnp.concatenate([w_down, ff_other[2 * ff_rows :]])

    own_positions = (
        lax.dynamic_slice_in_dim(block_position, 2 * ctx_rank, 2)[:, None] * half_block
        + jnp.arange(half_block, dtype=jnp.int32)[None, :]
    ).reshape(shard_rows)
    cosine_lookup, sine_lookup = rope_tables(own_positions, HEAD_DIM)
    row_positions = jnp.tile(own_positions, heads_per_group)
    scale_one = norm_scale(inputs)
    normed_one = (inputs * scale_one * gain_one).astype(BF16)
    normed_relative = matmul(normed_one, reorder).astype(BF16)
    projected = matmul(normed_relative, full_qkv) + bias_values
    value_lowered = projected[:, query_width + key_value_width :].astype(BF16)
    rotated_queries = apply_rotary(
        projected[:, :query_width].reshape(shard_rows, QUERY_HEADS, HEAD_DIM),
        cosine_lookup,
        sine_lookup,
    ).astype(BF16)
    rotated_keys = (
        apply_rotary(
            projected[:, query_width : query_width + key_value_width].reshape(
                shard_rows, KEY_VALUE_HEADS, HEAD_DIM
            ),
            cosine_lookup,
            sine_lookup,
        )
        .astype(BF16)
        .reshape(shard_rows, key_value_width)
    )
    key_value = jnp.concatenate([rotated_keys, value_lowered], axis=1)
    key_value = jnp.concatenate([key_value, grid.shift(key_value, dc=1)])
    places = [(jy_, jx_) for jy_ in range(y_count) for jx_ in range(x_count)]
    gathered = jnp.concatenate([grid.shift(key_value, dy=a, dx=b) for a, b in places])
    key_ctx = jnp.stack(
        [
            (((place_y - a) % y_count) * x_count + (place_x - b) % x_count) * CORES
            + (place_c - j) % CORES
            for a, b in places
            for j in range(CORES)
        ]
    )
    key_positions = (
        jnp.take(block_position.reshape(ctx_count, 2), key_ctx, axis=0)[:, :, None] * half_block
        + jnp.arange(half_block, dtype=jnp.int32)[None, None, :]
    ).reshape(shard_rows * ctx_count)
    seq_length = shard_rows * ctx_count
    all_keys = gathered[:, :key_value_width].reshape(seq_length, KEY_VALUE_HEADS, HEAD_DIM)
    all_values = gathered[:, key_value_width:].reshape(seq_length, KEY_VALUE_HEADS, HEAD_DIM)

    grad_chunks = grid.gather(after(grad_mid, weight_chunks[-1]))

    grouped_queries = (
        rotated_queries.reshape(shard_rows, KEY_VALUE_HEADS, heads_per_group, HEAD_DIM)
        .transpose(1, 2, 0, 3)
        .reshape(KEY_VALUE_HEADS, grouped_rows, HEAD_DIM)
    )
    visible = (key_positions[None, :] <= row_positions[:, None])[None]

    def attention_scores():
        raw = (
            jnp.einsum("hqd,khd->hqk", grouped_queries, all_keys, preferred_element_type=F32)
            * score_scale
        )
        return jnp.where(visible, raw, MASK_FILL)

    scores = attention_scores()
    row_peak = jnp.max(scores, axis=-1)
    log_total = row_peak + jnp.log(jnp.sum(jnp.exp(scores - row_peak[..., None]), axis=-1))
    soft = jnp.exp(scores - log_total[..., None])
    combined_heads = jnp.einsum(
        "hqk,khd->hqd", soft.astype(BF16), all_values, preferred_element_type=F32
    )
    attended = (
        combined_heads.reshape(KEY_VALUE_HEADS, heads_per_group, shard_rows, HEAD_DIM)
        .transpose(2, 0, 1, 3)
        .reshape(shard_rows, query_width)
        .astype(BF16)
    )
    attended_relative = matmul(attended, reorder).astype(BF16)
    hidden_one = inputs + matmul(attended_relative, full_output)
    scale_two = norm_scale(hidden_one)
    normed_two = (hidden_one * scale_two * gain_two).astype(BF16)

    normed_chunks = grid.gather(normed_two)
    hidden_parts, gate_parts, up_parts = [], [], []
    out_parts, normed_grad_parts = [], []
    for normed_chunk, grad_chunk in zip(normed_chunks, grad_chunks):
        gate_values = matmul_nt(normed_chunk, gate_pair)
        up_values = matmul_nt(normed_chunk, up_pair)
        grad_hidden = matmul_nt(grad_chunk, down_pair)
        sigmoid_gate = jax.nn.sigmoid(gate_values)
        active = gate_values * sigmoid_gate
        hidden = (active * up_values).astype(BF16)
        up_low = (grad_hidden * active).astype(BF16)
        gate_low = (
            grad_hidden * up_values * (sigmoid_gate * (1.0 + gate_values * (1.0 - sigmoid_gate)))
        ).astype(BF16)
        hidden_parts.append(hidden)
        gate_parts.append(gate_low)
        up_parts.append(up_low)
        out_parts.append(matmul(hidden, down_pair).astype(BF16))
        normed_grad_parts.append(
            (matmul(gate_low, gate_pair) + matmul(up_low, up_pair)).astype(BF16)
        )
    normed_all = jnp.concatenate(normed_chunks)
    grad_all = jnp.concatenate(grad_chunks)

    def own_rows(pair):
        other = grid.shift(pair[ff_rows:].astype(BF16), dc=1)
        return pair[:ff_rows] + other.astype(F32)

    grad_gate = own_rows(matmul_tn(jnp.concatenate(gate_parts), normed_all))
    grad_up = own_rows(matmul_tn(jnp.concatenate(up_parts), normed_all))
    grad_down = own_rows(matmul_tn(jnp.concatenate(hidden_parts), grad_all))
    moment_gate = MOMENTUM * momentum_gate + grad_gate
    moment_up = MOMENTUM * momentum_up + grad_up
    moment_down = MOMENTUM * momentum_down + grad_down

    ff_start = jnp.stack([m.astype(BF16) for m in (moment_gate, moment_up, moment_down)])
    ff_count = ff_start.shape[0]

    def weight_at(a, b):
        column = ((place_y + a) % y_count) * x_count + (place_x + b) % x_count
        return lax.dynamic_index_in_dim(
            ff_start, jnp.minimum(column, ff_count - 1), axis=0, keepdims=False
        )

    def has_weight(y, x):
        return y * x_count + x < ff_count

    current = jnp.concatenate(
        [grid.shift(weight_at(a, b), dy=a, dx=b, keep=has_weight) for a, b in places]
    )
    gram_part = matmul_tn(current, current).astype(BF16)
    half_rows = width // CORES
    kept = lax.dynamic_slice_in_dim(gram_part, place_c * half_rows, half_rows)
    sent = lax.dynamic_slice_in_dim(gram_part, (1 - place_c) * half_rows, half_rows)
    gram_half = (kept.astype(F32) + grid.shift(sent, dc=1).astype(F32)).astype(BF16)
    z_rows = half_rows // z_count
    gram_own = grid.z_sum(
        [
            lax.dynamic_slice_in_dim(gram_half, ((place_z - j) % z_count) * z_rows, z_rows)
            for j in range(z_count)
        ]
    ).astype(BF16)
    gram_half = jnp.zeros((half_rows, width), BF16)
    piece = gram_own
    for j in range(z_count):
        gram_half = lax.dynamic_update_slice_in_dim(
            gram_half, piece, ((place_z - j) % z_count) * z_rows, axis=0
        )
        if j + 1 < z_count:
            piece = grid.shift(piece, dz=1)
    gram_other = grid.shift(gram_half, dc=1)
    gram = jnp.where(
        place_c == 0,
        jnp.concatenate([gram_half, gram_other]),
        jnp.concatenate([gram_other, gram_half]),
    )
    moved = advance(current, *polynomials(gram.astype(F32)))
    back = jnp.stack(
        [
            grid.shift(moved[k * ff_rows : (k + 1) * ff_rows], dy=-a, dx=-b)
            for k, (a, b) in enumerate(places)
        ]
    )

    def ff_update(index):
        a = (index // x_count - place_y) % y_count
        b = (index % x_count - place_x) % x_count
        rows = lax.dynamic_index_in_dim(back, a * x_count + b, axis=0, keepdims=False)
        scale = -STEP_SCALE * math.sqrt(max(ff_rows * all_count, width))
        return scale * rows.astype(F32)

    update_gate, update_up, update_down = ff_update(0), ff_update(1), ff_update(2)

    grad_normed_two = grid.reduce(normed_grad_parts)
    grad_hidden_one, grad_gain_two = norm_back(hidden_one, scale_two, gain_two, grad_normed_two)
    grad_hidden_one = grad_hidden_one + grad_out
    grad_branch = grad_hidden_one.astype(BF16)
    attended_gradient = matmul_nt(
        matmul_nt(grad_branch, full_output).astype(BF16), reorder
    ).astype(BF16)
    grad_grouped = (
        attended_gradient.reshape(shard_rows, KEY_VALUE_HEADS, heads_per_group, HEAD_DIM)
        .transpose(1, 2, 0, 3)
        .reshape(KEY_VALUE_HEADS, grouped_rows, HEAD_DIM)
    )
    row_inner = jnp.sum(grad_grouped.astype(F32) * combined_heads, axis=-1)
    soft = jnp.exp(attention_scores() - log_total[..., None])
    grad_soft = jnp.einsum("hqd,khd->hqk", grad_grouped, all_values, preferred_element_type=F32)
    value_part = jnp.einsum(
        "hqk,hqd->khd", soft.astype(BF16), grad_grouped, preferred_element_type=F32
    )
    score_grad = (soft * (grad_soft - row_inner[..., None])).astype(BF16)
    query_part = jnp.einsum("hqk,khd->hqd", score_grad, all_keys, preferred_element_type=F32)
    key_part = jnp.einsum("hqk,hqd->khd", score_grad, grouped_queries, preferred_element_type=F32)
    key_value_grad = jnp.concatenate(
        [
            key_part.reshape(seq_length, key_value_width) * score_scale,
            value_part.reshape(seq_length, key_value_width),
        ],
        axis=1,
    ).astype(BF16)
    pair_rows = CORES * shard_rows
    pair_grad = sum(
        grid.shift(key_value_grad[k * pair_rows : (k + 1) * pair_rows], dy=-a, dx=-b).astype(F32)
        for k, (a, b) in enumerate(places)
    )
    key_value_sum = pair_grad[:shard_rows] + grid.shift(
        pair_grad[shard_rows:].astype(BF16), dc=1
    ).astype(F32)
    query_grad_heads = (
        (query_part * score_scale)
        .reshape(KEY_VALUE_HEADS, heads_per_group, shard_rows, HEAD_DIM)
        .transpose(2, 0, 1, 3)
        .reshape(shard_rows, QUERY_HEADS, HEAD_DIM)
    )
    query_grad_low = (
        apply_rotary(query_grad_heads, cosine_lookup, -sine_lookup)
        .astype(BF16)
        .reshape(shard_rows, query_width)
    )
    key_grad_low = (
        apply_rotary(
            key_value_sum[:, :key_value_width].reshape(shard_rows, KEY_VALUE_HEADS, HEAD_DIM),
            cosine_lookup,
            -sine_lookup,
        )
        .astype(BF16)
        .reshape(shard_rows, key_value_width)
    )
    value_grad_low = key_value_sum[:, key_value_width:].astype(BF16)
    qkv_grad_low = jnp.concatenate([query_grad_low, key_grad_low, value_grad_low], axis=1)

    weight_part = jnp.concatenate(
        [
            matmul_tn(normed_relative, qkv_grad_low).astype(BF16),
            matmul_tn(attended_relative, grad_branch).astype(BF16),
        ],
        axis=1,
    ).reshape(z_count, CORES, plane * weight_rows, qkv_width + width)
    other = grid.shift(weight_part[:, 1], dc=1)
    weight_sum = weight_part[:, 0].astype(F32) + other.astype(F32)
    attention_grads = grid.reduce([weight_sum[j].astype(BF16) for j in range(z_count)])
    grad_query = attention_grads[:, :query_width]
    grad_key = attention_grads[:, query_width : query_width + key_value_width]
    grad_value = attention_grads[:, query_width + key_value_width : qkv_width]
    grad_output = attention_grads[:, qkv_width:]

    normed_grad = matmul_nt(qkv_grad_low, full_qkv)
    high = normed_grad.astype(BF16)
    low = (normed_grad - high.astype(F32)).astype(BF16)
    grad_normed_one = matmul_nt(high, reorder) + matmul_nt(low, reorder)
    grad_inputs, grad_gain_one = norm_back(inputs, scale_one, gain_one, grad_normed_one)
    grad_tokens = (grad_inputs + grad_hidden_one)[None]
    vectors = lax.psum(
        jnp.concatenate(
            [jnp.sum(qkv_grad_low, axis=0, dtype=F32), grad_gain_one, grad_gain_two]
        ),
        ("ctx", "fsdp"),
    )
    grad_bias = vectors[:qkv_width]
    grad_gains = vectors[qkv_width:].reshape(2, width)
    moment_bias, update_bias = vector_step(bias_momentum, grad_bias)
    moment_gains, update_gains = vector_step(momentum_gains, grad_gains)

    moment_query = MOMENTUM * momentum_query + grad_query
    moment_key = MOMENTUM * key_momentum + grad_key
    moment_value = MOMENTUM * value_momentum + grad_value
    moment_output = MOMENTUM * momentum_output + grad_output
    query_key = jnp.concatenate([moment_query, moment_key], axis=1).astype(BF16)
    output_value = jnp.concatenate([moment_output, moment_value], axis=1).astype(BF16)
    mine = jnp.where(place_c == 0, query_key, output_value)
    theirs = jnp.where(place_c == 0, output_value, query_key)
    pair_start = jnp.concatenate([mine, grid.shift(theirs, dc=1)])
    start_all = jnp.concatenate(grid.gather(pair_start))
    large, small = start_all[:, :width], start_all[:, width:]
    large_new = advance(pair_start[:, :width], *polynomials(matmul_tn(large, large)))
    small_new = advance(pair_start[:, width:], *polynomials(matmul_tn(small, small)))
    pair_new = jnp.concatenate([large_new, small_new], axis=1)
    mine_new = pair_new[:weight_rows]
    theirs_new = grid.shift(pair_new[weight_rows:], dc=1)
    query_key_new = jnp.where(place_c == 0, mine_new, theirs_new).astype(F32)
    output_value_new = jnp.where(place_c == 0, theirs_new, mine_new).astype(F32)
    scale = -STEP_SCALE * math.sqrt(max(weight_rows * all_count, width))
    kv_scale = -STEP_SCALE * math.sqrt(max(weight_rows * all_count, key_value_width))
    update_query = scale * query_key_new[:, :width]
    update_key = kv_scale * query_key_new[:, width:]
    update_output = scale * output_value_new[:, :width]
    update_value = kv_scale * output_value_new[:, width:]

    out_tokens = (hidden_one + grid.reduce(out_parts)).astype(BF16)[None]
    return (
        out_tokens,
        grad_tokens,
        grad_query,
        grad_key,
        grad_value,
        grad_output,
        grad_gate,
        grad_up,
        grad_down,
        moment_query,
        moment_key,
        moment_value,
        moment_output,
        moment_gate,
        moment_up,
        moment_down,
        update_query,
        update_key,
        update_value,
        update_output,
        update_gate,
        update_up,
        update_down,
        grad_bias,
        moment_bias,
        update_bias,
        grad_gains,
        moment_gains,
        update_gains,
    )


def solution(mesh):
    tokens = P("fsdp", "ctx", None)
    rows = P(("ctx", "fsdp"), None)
    return jax.shard_map(
        shards,
        mesh=mesh,
        in_specs=(tokens, tokens, P()) + (rows,) * 7 + (P(), P()) + (rows,) * 7 + (P(), P()),
        out_specs=(tokens, tokens) + (rows,) * 21 + (P(),) * 6,
        check_vma=False,
    )
```

```python
import functools
import math

import jax
import jax.numpy as jnp
import numpy as np
from jax import lax
from jax.experimental import pallas as pl
from jax.experimental.pallas import tpu as pltpu
from jax.sharding import PartitionSpec as P

QUERY_HEADS = 12
KEY_VALUE_HEADS = 2
HEAD_DIM = 128
CORES = 2
TILE = 256
VMEM_BYTES = 56 * 2**20

NORM_EPSILON = 1e-06
ROPE_BASE = 1000000.0
POLY_ONE = 3.4445
POLY_THREE = -4.775
POLY_FIVE = 2.0315
MOMENTUM = 0.95
STEP_SCALE = 0.06
VECTOR_STEP = 0.1
MASK_FILL = -1e30

F32 = jnp.float32
BF16 = jnp.bfloat16


def matmul(left, right):
    return jnp.dot(left, right, preferred_element_type=F32)


def matmul_nt(left, right):
    return lax.dot_general(left, right, (((1,), (1,)), ((), ())), preferred_element_type=F32)


def matmul_tn(left, right):
    return lax.dot_general(left, right, (((0,), (0,)), ((), ())), preferred_element_type=F32)


def after(value, *others):
    return lax.optimization_barrier((value,) + others)[0]


class Grid:
    def __init__(self, ctx_count, z_count):
        plane = ctx_count // CORES
        x_count = math.isqrt(plane)
        while plane % x_count:
            x_count -= 1
        self.x_count, self.y_count, self.z_count = x_count, plane // x_count, z_count

    def place(self):
        ctx = lax.axis_index("ctx")
        return (
            ctx // (CORES * self.x_count),
            (ctx // CORES) % self.x_count,
            ctx % CORES,
            lax.axis_index("fsdp"),
        )

    def shift(self, value, dy=0, dx=0, dc=0, dz=0, dpair=0, dhigh=0, keep=None):
        y_count, x_count, z_count = self.y_count, self.x_count, self.z_count
        if dz or dpair or dhigh:
            pairs = []
            for z in range(z_count):
                high, low = (z // 2 + dhigh) % (z_count // 2), (z % 2 + dpair) % 2
                pairs.append((z, (high * 2 + low + dz) % z_count))
            return lax.ppermute(value, "fsdp", pairs)
        dy, dx, dc = dy % y_count, dx % x_count, dc % CORES
        if not (dy or dx or dc):
            return value
        pairs = []
        for y in range(y_count):
            for x in range(x_count):
                for c in range(CORES):
                    to_y, to_x, to_c = (y + dy) % y_count, (x + dx) % x_count, (c + dc) % CORES
                    if keep is None or keep(to_y, to_x):
                        pairs.append(
                            ((y * x_count + x) * CORES + c, (to_y * x_count + to_x) * CORES + to_c)
                        )
        return lax.ppermute(value, "ctx", pairs)

    def plane_gather(self, block):
        half = block.shape[0] // 2
        first, second = block[:half], block[half:]
        first = jnp.concatenate(
            [first] + [self.shift(first, dx=j) for j in range(1, self.x_count)]
        )
        second = jnp.concatenate(
            [second] + [self.shift(second, dy=j) for j in range(1, self.y_count)]
        )
        return jnp.concatenate(
            [first]
            + [self.shift(first, dy=j) for j in range(1, self.y_count)]
            + [second]
            + [self.shift(second, dx=j) for j in range(1, self.x_count)]
        )

    def plane_order(self, rows):
        half = rows // 2
        jy, jx, row = [], [], []
        for y in range(self.y_count):
            for x in range(self.x_count):
                for r in range(half):
                    jy.append(y), jx.append(x), row.append(r)
        for x in range(self.x_count):
            for y in range(self.y_count):
                for r in range(half, rows):
                    jy.append(y), jx.append(x), row.append(r)
        return np.array(jy), np.array(jx), np.array(row)

    def z_slots(self, block):
        return [block] + [self.shift(block, dz=j) for j in range(1, self.z_count)]

    def gather(self, slots):
        size = self.z_count // 2
        return [
            self.plane_gather(jnp.concatenate(slots[k : k + size]))
            for k in range(0, self.z_count, size)
        ]

    def gather_order(self, rows):
        size = self.z_count // 2
        jy, jx, row = self.plane_order(size * rows)
        jz = [k + row // rows for k in range(0, self.z_count, size)]
        return jz, jy, jx, row % rows

    def plane_reduce(self, part):
        def step(rows, count, axis):
            size = rows.shape[0] // count
            total = rows[:size].astype(F32)
            for j in range(1, count):
                piece = rows[j * size : (j + 1) * size].astype(BF16)
                total = total + self.shift(piece, **{axis: -j}).astype(F32)
            return total

        half = part.shape[0] // 2
        first = step(step(part[:half], self.y_count, "dy"), self.x_count, "dx")
        second = step(step(part[half:], self.x_count, "dx"), self.y_count, "dy")
        return jnp.concatenate([first, second])

    def z_sum(self, parts):
        total = parts[0].astype(F32)
        for j in range(1, self.z_count):
            total = total + self.shift(parts[j].astype(BF16), dz=-j).astype(F32)
        return total

    def reduce_plane(self, parts):
        slots = []
        for part in parts:
            total = self.plane_reduce(part)
            size = self.z_count // len(parts)
            rows = total.shape[0] // size
            slots += [total[k * rows : (k + 1) * rows] for k in range(size)]
        return slots

    def token_gather(self, block):
        slots = [block] + [self.shift(block, dhigh=j) for j in range(1, self.z_count // 2)]
        return [self.plane_gather(slot) for slot in slots]

    def token_reduce(self, parts):
        terms = [self.plane_reduce(parts[0])]
        for j in range(1, len(parts)):
            piece = self.plane_reduce(parts[j]).astype(BF16)
            terms.append(self.shift(piece, dhigh=-j))
        return terms

    def total(self, value):
        for axis, count in (("ctx", self.y_count * self.x_count * CORES), ("fsdp", self.z_count)):
            step = 1
            while step < count:
                value = value + lax.ppermute(value, axis, [(k, k ^ step) for k in range(count)])
                step *= 2
        return value


def rope_tables(positions, head_size):
    half_width = head_size // 2
    ratios = jnp.arange(half_width, dtype=F32) * (2.0 / head_size)
    frequency = jnp.exp(-math.log(ROPE_BASE) * ratios)
    angles = positions.astype(F32)[:, None] * frequency[None, :]
    cosine, sine = jnp.cos(angles), jnp.sin(angles)
    return jnp.concatenate([cosine, cosine], axis=1), jnp.concatenate([-sine, sine], axis=1)


def norm_scale(values):
    return lax.rsqrt(jnp.mean(values * values, axis=-1, keepdims=True) + NORM_EPSILON)


def norm_back(values, scale_rows, gain, grad_normed):
    weighted = grad_normed * gain
    inner_mean = jnp.mean(weighted * values, axis=-1, keepdims=True)
    grad_values = (
        scale_rows * weighted - values * (scale_rows * scale_rows * scale_rows) * inner_mean
    )
    grad_gain = jnp.sum(grad_normed * values * scale_rows, axis=0, keepdims=True)
    return (grad_values, grad_gain)


def rotate(head, cosine, sine):
    return head * cosine + pltpu.roll(head, HEAD_DIM // 2, 1) * sine


def head_columns(head):
    return slice(head * HEAD_DIM, (head + 1) * HEAD_DIM)


def by_pieces(rows, piece_refs):
    total, start = 0.0, 0
    for ref in piece_refs:
        size = ref.shape[0]
        total = total + matmul(rows[:, start : start + size], ref[...])
        start += size
    return total


def by_pieces_nt(rows, piece_refs):
    return jnp.concatenate([matmul_nt(rows, ref[...]) for ref in piece_refs], axis=1)


def compute(kernel, outs, args, flops, scratch=()):
    return pl.pallas_call(
        kernel,
        out_shape=[jax.ShapeDtypeStruct(shape, dtype) for shape, dtype in outs],
        scratch_shapes=scratch,
        compiler_params=pltpu.CompilerParams(vmem_limit_bytes=VMEM_BYTES),
        cost_estimate=pl.CostEstimate(flops=flops, bytes_accessed=2**20, transcendentals=0),
    )(*args)


def project_kernel(
    tokens_ref, gains_ref, bias_ref, cosine_ref, sine_ref, reorder_ref, *refs
):
    piece_refs, (normed_ref, query_ref, key_value_ref) = refs[:-3], refs[-3:]
    inputs = tokens_ref[...].astype(F32)
    normed = (inputs * norm_scale(inputs) * gains_ref[0:1, :].astype(F32)).astype(BF16)
    normed = matmul(normed, reorder_ref[...]).astype(BF16)
    normed_ref[...] = normed
    projected = by_pieces(normed, piece_refs) + bias_ref[...].astype(F32)
    cosine, sine = cosine_ref[...], sine_ref[...]
    for head in range(QUERY_HEADS):
        rotated = rotate(projected[:, head_columns(head)], cosine, sine)
        query_ref[:, head_columns(head)] = rotated.astype(BF16)
    for head in range(2 * KEY_VALUE_HEADS):
        values = projected[:, head_columns(QUERY_HEADS + head)]
        if head < KEY_VALUE_HEADS:
            values = rotate(values, cosine, sine)
        key_value_ref[:, head_columns(head)] = values.astype(BF16)


def attend_kernel(piece_count, tokens_ref, gains_ref, reorder_ref, query_ref, rows_ref, keys_ref, *refs):
    key_value_refs, refs = refs[:piece_count], refs[piece_count:]
    weight_refs, refs = refs[:-6], refs[-6:]
    mixed_ref, log_ref, attended_ref, hidden_ref, normed_ref, all_ref = refs
    size = key_value_refs[0].shape[0]
    for k, ref in enumerate(key_value_refs):
        all_ref[k * size : (k + 1) * size, :] = ref[...]
    visible = keys_ref[...] <= rows_ref[...]
    scale = 1.0 / math.sqrt(HEAD_DIM)
    group = QUERY_HEADS // KEY_VALUE_HEADS
    attended = []
    log_ref[...] = jnp.zeros(log_ref.shape, F32)
    for head in range(QUERY_HEADS):
        keys = all_ref[:, head_columns(head // group)]
        values = all_ref[:, head_columns(KEY_VALUE_HEADS + head // group)]
        scores = matmul_nt(query_ref[:, head_columns(head)], keys) * scale
        scores = jnp.where(visible, scores, MASK_FILL)
        peak = jnp.max(scores, axis=-1, keepdims=True)
        weights = jnp.exp(scores - peak)
        total = jnp.sum(weights, axis=-1, keepdims=True)
        log_ref[:, head : head + 1] = peak + jnp.log(total)
        mixed = matmul((weights * (1.0 / total)).astype(BF16), values)
        mixed_ref[:, head_columns(head)] = mixed
        attended.append(mixed.astype(BF16))
    attended = jnp.concatenate(attended, axis=1)
    attended = matmul(attended, reorder_ref[...]).astype(BF16)
    attended_ref[...] = attended
    hidden = tokens_ref[...].astype(F32) + by_pieces(attended, weight_refs)
    hidden_ref[...] = hidden
    normed_ref[...] = (hidden * norm_scale(hidden) * gains_ref[1:2, :].astype(F32)).astype(BF16)


def attend_back_kernel(
    piece_count,
    grad_count,
    cotangent_ref,
    gains_ref,
    hidden_ref,
    reorder_ref,
    query_ref,
    rows_ref,
    keys_ref,
    cosine_ref,
    sine_ref,
    mixed_ref,
    log_ref,
    *refs,
):
    grad_refs, refs = refs[:grad_count], refs[grad_count:]
    key_value_refs, refs = refs[:piece_count], refs[piece_count:]
    outs = 4 + piece_count
    weight_refs, refs = refs[: -outs - 3], refs[-outs - 3 :]
    hidden_grad_ref, branch_ref, gain_ref, query_grad_ref = refs[:4]
    piece_refs, (all_ref, key_sum, value_sum) = refs[4:outs], refs[outs:]
    size = key_value_refs[0].shape[0]
    for k, ref in enumerate(key_value_refs):
        all_ref[k * size : (k + 1) * size, :] = ref[...]
    hidden = hidden_ref[...]
    grad_normed = sum(ref[...].astype(F32) for ref in grad_refs)
    grad, grad_gain = norm_back(
        hidden, norm_scale(hidden), gains_ref[1:2, :].astype(F32), grad_normed
    )
    gain_ref[...] = grad_gain
    grad = grad + cotangent_ref[...].astype(F32)
    hidden_grad_ref[...] = grad
    branch = grad.astype(BF16)
    branch_ref[...] = branch
    attended_grad = by_pieces_nt(branch, weight_refs).astype(BF16)
    attended_grad = matmul_nt(attended_grad, reorder_ref[...]).astype(BF16)
    visible = keys_ref[...] <= rows_ref[...]
    scale = 1.0 / math.sqrt(HEAD_DIM)
    group = QUERY_HEADS // KEY_VALUE_HEADS
    cosine, sine = cosine_ref[...], sine_ref[...]
    for head in range(QUERY_HEADS):
        kind = head // group
        keys = all_ref[:, head_columns(kind)]
        values = all_ref[:, head_columns(KEY_VALUE_HEADS + kind)]
        query = query_ref[:, head_columns(head)]
        own = attended_grad[:, head_columns(head)]
        scores = matmul_nt(query, keys) * scale
        soft = jnp.exp(jnp.where(visible, scores, MASK_FILL) - log_ref[:, head : head + 1])
        inner = jnp.sum(
            own.astype(F32) * mixed_ref[:, head_columns(head)], axis=-1, keepdims=True
        )
        score_grad = (soft * (matmul_nt(own, values) - inner)).astype(BF16)
        query_grad = matmul(score_grad, keys) * scale
        query_grad_ref[:, head_columns(head)] = rotate(query_grad, cosine, -sine).astype(BF16)
        key_part = matmul_tn(score_grad, query)
        value_part = matmul_tn(soft.astype(BF16), own)
        if head % group == 0:
            key_sum[...] = key_part
            value_sum[...] = value_part
        else:
            key_sum[...] += key_part
            value_sum[...] += value_part
        if head % group == group - 1:
            for k, ref in enumerate(piece_refs):
                rows = slice(k * size, (k + 1) * size)
                ref[:, head_columns(kind)] = (key_sum[rows, :] * scale).astype(BF16)
                ref[:, head_columns(KEY_VALUE_HEADS + kind)] = value_sum[rows, :].astype(BF16)


def weights_back_kernel(
    tokens_ref,
    gains_ref,
    reorder_ref,
    cosine_ref,
    sine_ref,
    normed_ref,
    attended_ref,
    branch_ref,
    hidden_grad_ref,
    query_grad_ref,
    pair_ref,
    other_ref,
    *refs,
):
    weight_refs, refs = refs[:-6], refs[-6:]
    own_ref, sent_ref, tokens_grad_ref, bias_ref, gain_ref, grad_ref = refs
    query_width = query_grad_ref.shape[1]
    grad_ref[:, :query_width] = query_grad_ref[...]
    key_value = pair_ref[...] + other_ref[...].astype(F32)
    cosine, sine = cosine_ref[...], sine_ref[...]
    for head in range(2 * KEY_VALUE_HEADS):
        values = key_value[:, head_columns(head)]
        if head < KEY_VALUE_HEADS:
            values = rotate(values, cosine, -sine)
        grad_ref[:, head_columns(QUERY_HEADS + head)] = values.astype(BF16)
    grad = grad_ref[...]
    bias_ref[...] = jnp.sum(grad.astype(F32), axis=0, keepdims=True)
    qkv_width = grad.shape[1]
    branch = branch_ref[...]
    size = own_ref.shape[1]
    for k in range(2 * CORES):
        out = sent_ref if k % CORES else own_ref
        rows = slice(k * size, (k + 1) * size)
        out[k // CORES, :, :qkv_width] = matmul_tn(normed_ref[:, rows], grad).astype(BF16)
        out[k // CORES, :, qkv_width:] = matmul_tn(attended_ref[:, rows], branch).astype(BF16)
    normed_grad = by_pieces_nt(grad, weight_refs)
    high = normed_grad.astype(BF16)
    low = (normed_grad - high.astype(F32)).astype(BF16)
    reorder = reorder_ref[...]
    normed_grad = matmul_nt(high, reorder) + matmul_nt(low, reorder)
    inputs = tokens_ref[...].astype(F32)
    grad, grad_gain = norm_back(
        inputs, norm_scale(inputs), gains_ref[0:1, :].astype(F32), normed_grad
    )
    gain_ref[...] = grad_gain
    tokens_grad_ref[...] = grad + hidden_grad_ref[...]


def vector_step(old_state, gradient):
    fresh_state = MOMENTUM * old_state + gradient
    inverse_rms = lax.rsqrt(
        jnp.mean(fresh_state * fresh_state, axis=-1, keepdims=True) + NORM_EPSILON
    )
    return (fresh_state, -VECTOR_STEP * fresh_state * inverse_rms)


def packed_height(width):
    count = width // TILE
    return count * (count + 1) // 2 * TILE


def packed_block(row, column, count):
    return pl.ds((row * count - row * (row - 1) // 2 + column - row) * TILE, TILE)


def block_rows(index):
    return slice(index * TILE, (index + 1) * TILE)


def gram_kernel(start_ref, packed_ref):
    count = start_ref.shape[1] // TILE
    for i in range(count):
        row = lax.dot_general(
            start_ref[:, block_rows(i)],
            start_ref[:, i * TILE :],
            (((0,), (0,)), ((), ())),
            preferred_element_type=F32,
        )
        for j in range(i, count):
            packed_ref[packed_block(i, j, count), :] = row[:, block_rows(j - i)].astype(
                packed_ref.dtype
            )


def gram_packed(start, dtype):
    rows, width = start.shape
    height = packed_height(width)
    return pl.pallas_call(
        gram_kernel,
        out_shape=jax.ShapeDtypeStruct((height, TILE), dtype),
        compiler_params=pltpu.CompilerParams(vmem_limit_bytes=VMEM_BYTES),
        cost_estimate=pl.CostEstimate(
            flops=rows * width * width,
            bytes_accessed=2 * rows * width + 4 * height * TILE,
            transcendentals=0,
        ),
    )(start)


def chain_kernel(packed_ref, start_ref, new_ref, low, poly, mixed, two):
    count = start_ref.shape[1] // TILE

    def put(ref, i, j, block):
        ref[block_rows(i), block_rows(j)] = block
        if i != j:
            ref[block_rows(j), block_rows(i)] = block.T

    def product(left, right):
        for i in range(count):
            row = jnp.dot(left[block_rows(i), :], right[:, i * TILE :], preferred_element_type=F32)
            for j in range(i, count):
                yield i, j, row[:, block_rows(j - i)]

    same = lax.broadcasted_iota(jnp.int32, (TILE, TILE), 0) == lax.broadcasted_iota(
        jnp.int32, (TILE, TILE), 1
    )
    trace = jnp.zeros((1, 1), F32)
    for i in range(count):
        block = packed_ref[packed_block(i, i, count), :].astype(F32)
        trace = trace + jnp.sum(jnp.where(same, block, 0.0), keepdims=True)
    factor = 1.0 / (jnp.sqrt(trace) + 1e-07)
    square = factor * factor

    def gram_one(i, j):
        return packed_ref[packed_block(i, j, count), :].astype(F32) * square

    for i in range(count):
        for j in range(i, count):
            put(low, i, j, gram_one(i, j).astype(BF16))
    for i, j, block in product(low, low):
        put(poly, i, j, (POLY_THREE * gram_one(i, j) + POLY_FIVE * block).astype(BF16))
    for i, j, block in product(low, poly):
        two[packed_block(i, j, count), :] = (POLY_ONE * POLY_ONE) * gram_one(i, j) + (
            2.0 * POLY_ONE
        ) * block
        put(mixed, i, j, block.astype(BF16))
    for i, j, block in product(poly, mixed):
        block = two[packed_block(i, j, count), :] + block
        two[packed_block(i, j, count), :] = block
        put(low, i, j, block.astype(BF16))
    start = start_ref[...]
    middle = jnp.dot(start, poly[...], preferred_element_type=F32)
    middle = (factor * (POLY_ONE * start.astype(F32) + middle)).astype(BF16)
    for i, j, block in product(low, low):
        block = POLY_THREE * two[packed_block(i, j, count), :] + POLY_FIVE * block
        put(mixed, i, j, block.astype(BF16))
    new = jnp.dot(middle, mixed[...], preferred_element_type=F32)
    new_ref[...] = (POLY_ONE * middle.astype(F32) + new).astype(BF16)


def orthogonalize(packed, start):
    rows, width = start.shape
    return pl.pallas_call(
        chain_kernel,
        out_shape=jax.ShapeDtypeStruct(start.shape, BF16),
        scratch_shapes=[
            pltpu.VMEM((width, width), BF16),
            pltpu.VMEM((width, width), BF16),
            pltpu.VMEM((width, width), BF16),
            pltpu.VMEM((packed_height(width), TILE), F32),
        ],
        compiler_params=pltpu.CompilerParams(vmem_limit_bytes=VMEM_BYTES),
        cost_estimate=pl.CostEstimate(
            flops=5 * width**3 + 4 * rows * width * width,
            bytes_accessed=4 * rows * width + 4 * packed_height(width) * TILE,
            transcendentals=0,
        ),
    )(packed, start)


def shards(
    tokens,
    cotangent,
    block_position,
    w_query,
    key_weight,
    value_weight,
    w_output,
    w_gate,
    w_up,
    w_down,
    projection_bias,
    norm_gains,
    momentum_query,
    key_momentum,
    value_momentum,
    momentum_output,
    momentum_gate,
    momentum_up,
    momentum_down,
    bias_momentum,
    momentum_gains,
):
    shard_rows = tokens.shape[1]
    width = tokens.shape[2]
    ctx_count = lax.axis_size("ctx")
    z_count = lax.axis_size("fsdp")
    grid = Grid(ctx_count, z_count)
    y_count, x_count = grid.y_count, grid.x_count
    plane = y_count * x_count
    place_y, place_x, place_c, place_z = grid.place()
    ctx_rank = lax.axis_index("ctx")
    all_count = ctx_count * z_count
    half_block = shard_rows // 2
    query_width = QUERY_HEADS * HEAD_DIM
    key_value_width = KEY_VALUE_HEADS * HEAD_DIM
    weight_rows = w_query.shape[0]
    ff_rows = w_gate.shape[0]

    def both_cores(chunks):
        parts = []
        for chunk in chunks:
            parts += [chunk, grid.shift(chunk, dc=1)]
        return parts

    qkv_width = query_width + 2 * key_value_width
    qkv_slots = grid.z_slots(jnp.concatenate([w_query, key_weight, value_weight], axis=1))
    qkv_chunks = grid.gather(qkv_slots)
    qkv_pieces = both_cores(qkv_chunks)
    output_slots = grid.z_slots(after(w_output, qkv_slots[-1]))
    output_chunks = grid.gather(after(output_slots, *qkv_chunks))
    output_pieces = both_cores(output_chunks)
    tokens = after(tokens, qkv_slots[-1])
    place_y, place_x, place_c, place_z = after(
        (place_y, place_x, place_c, place_z), qkv_slots[-1]
    )
    jz_parts, jy, jx, row = grid.gather_order(weight_rows)
    source_y = (place_y - jnp.asarray(jy)) % y_count
    source_x = (place_x - jnp.asarray(jx)) % x_count
    pieces = []
    for jz in jz_parts:
        source_z = (place_z - jnp.asarray(jz)) % z_count
        for jc in range(CORES):
            source_ctx = (source_y * x_count + source_x) * CORES + (place_c - jc) % CORES
            pieces.append((source_ctx * z_count + source_z) * weight_rows + jnp.asarray(row))
    relative_rows = jnp.concatenate(pieces)
    reorder = (jnp.arange(width, dtype=jnp.int32)[:, None] == relative_rows[None, :]).astype(BF16)

    own_tokens = tokens[0]
    grad_mid = cotangent[0]

    own_positions = (
        lax.dynamic_slice_in_dim(block_position, 2 * ctx_rank, 2)[:, None] * half_block
        + jnp.arange(half_block, dtype=jnp.int32)[None, :]
    ).reshape(shard_rows)
    cosine_lookup, sine_lookup = rope_tables(own_positions, HEAD_DIM)
    row_positions = own_positions[:, None]
    normed_relative, queries, key_value = compute(
        project_kernel,
        [
            ((shard_rows, width), BF16),
            ((shard_rows, query_width), BF16),
            ((shard_rows, 2 * key_value_width), BF16),
        ],
        [
            own_tokens,
            norm_gains,
            projection_bias[None, :],
            cosine_lookup,
            sine_lookup,
            reorder,
            *qkv_pieces,
        ],
        2 * shard_rows * width * qkv_width,
    )
    key_value_pair = jnp.concatenate([key_value, grid.shift(key_value, dc=1)])
    places = [(jy_, jx_) for jy_ in range(y_count) for jx_ in range(x_count)]
    key_value_pieces = [grid.shift(key_value_pair, dy=a, dx=b) for a, b in places]
    key_ctx = jnp.stack(
        [
            (((place_y - a) % y_count) * x_count + (place_x - b) % x_count) * CORES
            + (place_c - j) % CORES
            for a, b in places
            for j in range(CORES)
        ]
    )
    key_positions = (
        jnp.take(block_position.reshape(ctx_count, 2), key_ctx, axis=0)[:, :, None] * half_block
        + jnp.arange(half_block, dtype=jnp.int32)[None, None, :]
    ).reshape(1, shard_rows * ctx_count)
    seq_length = shard_rows * ctx_count

    shared = 2 * CORES
    ff_block = after(jnp.concatenate([w_gate, w_up, w_down]), qkv_slots[-1], output_slots[-1])
    ff_chip = jnp.concatenate([ff_block, grid.shift(ff_block, dpair=1)])
    ff_chip = after(ff_chip, key_value)
    ff_all = jnp.concatenate([ff_chip, grid.shift(ff_chip, dc=1)])
    ff_all = ff_all.reshape(shared, 3, ff_rows, width)
    gate_shared, up_shared, down_shared = (
        ff_all[:, k].reshape(shared * ff_rows, width) for k in range(3)
    )

    grad_chunks = grid.token_gather(after(grad_mid, output_chunks[-1]))

    mixed, log_total, attended_relative, hidden_one, normed_two = compute(
        functools.partial(attend_kernel, plane),
        [
            ((shard_rows, query_width), F32),
            ((shard_rows, HEAD_DIM), F32),
            ((shard_rows, query_width), BF16),
            ((shard_rows, width), F32),
            ((shard_rows, width), BF16),
        ],
        [
            own_tokens,
            norm_gains,
            reorder,
            queries,
            row_positions,
            key_positions,
            *key_value_pieces,
            *output_pieces,
        ],
        4 * shard_rows * width * width,
        [pltpu.VMEM((seq_length, 2 * key_value_width), BF16)],
    )

    normed_chunks = grid.token_gather(normed_two)
    out_parts, normed_grad_parts = [], []
    gate_sum = up_sum = down_sum = 0.0
    for normed_chunk, grad_chunk in zip(normed_chunks, grad_chunks):
        gate_values = matmul_nt(normed_chunk, gate_shared)
        up_values = matmul_nt(normed_chunk, up_shared)
        grad_hidden = matmul_nt(grad_chunk, down_shared)
        sigmoid_gate = jax.nn.sigmoid(gate_values)
        active = gate_values * sigmoid_gate
        hidden = (active * up_values).astype(BF16)
        up_low = (grad_hidden * active).astype(BF16)
        gate_low = (
            grad_hidden * up_values * (sigmoid_gate * (1.0 + gate_values * (1.0 - sigmoid_gate)))
        ).astype(BF16)
        normed_grad_parts.append(
            (matmul(gate_low, gate_shared) + matmul(up_low, up_shared)).astype(BF16)
        )
        gate_sum = gate_sum + matmul_tn(gate_low, normed_chunk)
        up_sum = up_sum + matmul_tn(up_low, normed_chunk)
        down_sum = down_sum + matmul_tn(hidden, grad_chunk)
        out_parts.append(matmul(hidden, down_shared).astype(BF16))

    def own_rows(total):
        chip_rows = 2 * ff_rows
        other = grid.shift(total[chip_rows:].astype(BF16), dc=1)
        chip_sum = total[:chip_rows] + other.astype(F32)
        piece = grid.shift(chip_sum[ff_rows:].astype(BF16), dpair=1)
        return chip_sum[:ff_rows] + piece.astype(F32)

    grad_gate, grad_up, grad_down = own_rows(gate_sum), own_rows(up_sum), own_rows(down_sum)
    moment_gate = MOMENTUM * momentum_gate + grad_gate
    moment_up = MOMENTUM * momentum_up + grad_up
    moment_down = MOMENTUM * momentum_down + grad_down

    normed_grad_sums = grid.token_reduce(normed_grad_parts)
    hidden_grad, grad_branch, grad_gain_two, query_grad, *key_value_grads = compute(
        functools.partial(attend_back_kernel, plane, len(normed_grad_sums)),
        [
            ((shard_rows, width), F32),
            ((shard_rows, width), BF16),
            ((1, width), F32),
            ((shard_rows, query_width), BF16),
        ]
        + [((CORES * shard_rows, 2 * key_value_width), BF16)] * plane,
        [
            grad_mid,
            norm_gains,
            hidden_one,
            reorder,
            queries,
            row_positions,
            key_positions,
            cosine_lookup,
            sine_lookup,
            mixed,
            log_total,
            *normed_grad_sums,
            *key_value_pieces,
            *output_pieces,
        ],
        4 * shard_rows * width * width,
        [
            pltpu.VMEM((seq_length, 2 * key_value_width), BF16),
            pltpu.VMEM((seq_length, HEAD_DIM), F32),
            pltpu.VMEM((seq_length, HEAD_DIM), F32),
        ],
    )
    pair_grad = sum(
        grid.shift(piece, dy=-a, dx=-b).astype(F32)
        for piece, (a, b) in zip(key_value_grads, places)
    )
    key_value_other = grid.shift(pair_grad[shard_rows:].astype(BF16), dc=1)

    weight_shape = (2, weight_rows * all_count // (2 * CORES), qkv_width + width)
    weight_own, weight_sent, grad_tokens, bias_term, grad_gain_one = compute(
        weights_back_kernel,
        [
            (weight_shape, BF16),
            (weight_shape, BF16),
            ((shard_rows, width), F32),
            ((1, qkv_width), F32),
            ((1, width), F32),
        ],
        [
            own_tokens,
            norm_gains,
            reorder,
            cosine_lookup,
            sine_lookup,
            normed_relative,
            attended_relative,
            grad_branch,
            hidden_grad,
            query_grad,
            pair_grad[:shard_rows],
            key_value_other,
            *qkv_pieces,
        ],
        4 * shard_rows * width * qkv_width,
        [pltpu.VMEM((shard_rows, qkv_width), BF16)],
    )
    other = grid.shift(weight_sent, dc=1)
    weight_sum = (weight_own.astype(F32) + other.astype(F32)).astype(BF16)
    attention_slots = grid.reduce_plane([weight_sum[j] for j in range(2)])
    attention_grads = grid.z_sum(attention_slots)
    grad_query = attention_grads[:, :query_width]
    grad_key = attention_grads[:, query_width : query_width + key_value_width]
    grad_value = attention_grads[:, query_width + key_value_width : qkv_width]
    grad_output = attention_grads[:, qkv_width:]

    vectors = grid.total(
        jnp.concatenate([bias_term, grad_gain_one, grad_gain_two], axis=1).reshape(-1, HEAD_DIM)
    ).reshape(-1)
    grad_bias = vectors[:qkv_width]
    grad_gains = vectors[qkv_width:].reshape(2, width)
    moment_bias, update_bias = vector_step(bias_momentum, grad_bias)
    moment_gains, update_gains = vector_step(momentum_gains, grad_gains)

    moment_query = MOMENTUM * momentum_query + grad_query
    moment_key = MOMENTUM * key_momentum + grad_key
    moment_value = MOMENTUM * value_momentum + grad_value
    moment_output = MOMENTUM * momentum_output + grad_output
    query_key = jnp.concatenate([moment_query, moment_key], axis=1).astype(BF16)
    output_value = jnp.concatenate([moment_output, moment_value], axis=1).astype(BF16)
    mine = jnp.where(place_c == 0, query_key, output_value)
    theirs = jnp.where(place_c == 0, output_value, query_key)
    pair_start = jnp.concatenate([mine, grid.shift(theirs, dc=1)])
    start_slots = grid.z_slots(pair_start)
    start_all = jnp.concatenate(grid.gather(start_slots))

    ff_start = jnp.stack([m.astype(BF16) for m in (moment_gate, moment_up, moment_down)])
    ff_start = after(ff_start, *attention_slots)
    ff_count = ff_start.shape[0]

    def weight_at(a, b):
        column = ((place_y + a) % y_count) * x_count + (place_x + b) % x_count
        return lax.dynamic_index_in_dim(
            ff_start, jnp.minimum(column, ff_count - 1), axis=0, keepdims=False
        )

    def has_weight(y, x):
        return y * x_count + x < ff_count

    current = jnp.concatenate(
        [grid.shift(weight_at(a, b), dy=a, dx=b, keep=has_weight) for a, b in places]
    )
    current = after(current, pair_start)
    gram_part = gram_packed(current, BF16)
    half_rows = gram_part.shape[0] // CORES
    kept = lax.dynamic_slice_in_dim(gram_part, place_c * half_rows, half_rows)
    sent = lax.dynamic_slice_in_dim(gram_part, (1 - place_c) * half_rows, half_rows)
    gram_half = (kept.astype(F32) + grid.shift(sent, dc=1).astype(F32)).astype(BF16)
    gram_half = after(gram_half, *start_slots)
    z_rows = half_rows // z_count
    gram_own = grid.z_sum(
        [
            lax.dynamic_slice_in_dim(gram_half, ((place_z - j) % z_count) * z_rows, z_rows)
            for j in range(z_count)
        ]
    ).astype(BF16)
    gram_half = jnp.zeros((half_rows, TILE), BF16)
    for j, piece in enumerate(grid.z_slots(gram_own)):
        gram_half = lax.dynamic_update_slice_in_dim(
            gram_half, piece, ((place_z - j) % z_count) * z_rows, axis=0
        )
    gram_other = grid.shift(gram_half, dc=1)
    gram = jnp.where(
        place_c == 0,
        jnp.concatenate([gram_half, gram_other]),
        jnp.concatenate([gram_other, gram_half]),
    )
    moved = orthogonalize(after(gram, start_all), current)
    back = jnp.stack(
        [
            grid.shift(moved[k * ff_rows : (k + 1) * ff_rows], dy=-a, dx=-b)
            for k, (a, b) in enumerate(places)
        ]
    )

    def ff_update(index):
        a = (index // x_count - place_y) % y_count
        b = (index % x_count - place_x) % x_count
        rows = lax.dynamic_index_in_dim(back, a * x_count + b, axis=0, keepdims=False)
        scale = -STEP_SCALE * math.sqrt(max(ff_rows * all_count, width))
        return scale * rows.astype(F32)

    update_gate, update_up, update_down = ff_update(0), ff_update(1), ff_update(2)

    start_all = after(start_all, moved)
    large, small = start_all[:, :width], start_all[:, width:]
    large_new = orthogonalize(gram_packed(large, F32), pair_start[:, :width])
    small_new = orthogonalize(gram_packed(small, F32), pair_start[:, width:])
    pair_new = jnp.concatenate([large_new, small_new], axis=1)
    mine_new = pair_new[:weight_rows]
    theirs_new = grid.shift(pair_new[weight_rows:], dc=1)
    query_key_new = jnp.where(place_c == 0, mine_new, theirs_new).astype(F32)
    output_value_new = jnp.where(place_c == 0, theirs_new, mine_new).astype(F32)
    scale = -STEP_SCALE * math.sqrt(max(weight_rows * all_count, width))
    kv_scale = -STEP_SCALE * math.sqrt(max(weight_rows * all_count, key_value_width))
    update_query = scale * query_key_new[:, :width]
    update_key = kv_scale * query_key_new[:, width:]
    update_output = scale * output_value_new[:, :width]
    update_value = kv_scale * output_value_new[:, width:]

    out_terms = grid.token_reduce([after(part, pair_grad) for part in out_parts])
    out_tokens = sum((term.astype(F32) for term in out_terms), hidden_one).astype(BF16)[None]
    return (
        out_tokens,
        grad_tokens[None],
        grad_query,
        grad_key,
        grad_value,
        grad_output,
        grad_gate,
        grad_up,
        grad_down,
        moment_query,
        moment_key,
        moment_value,
        moment_output,
        moment_gate,
        moment_up,
        moment_down,
        update_query,
        update_key,
        update_value,
        update_output,
        update_gate,
        update_up,
        update_down,
        grad_bias,
        moment_bias,
        update_bias,
        grad_gains,
        moment_gains,
        update_gains,
    )


def solution(mesh):
    tokens = P("fsdp", "ctx", None)
    rows = P(("ctx", "fsdp"), None)
    return jax.shard_map(
        shards,
        mesh=mesh,
        in_specs=(tokens, tokens, P()) + (rows,) * 7 + (P(), P()) + (rows,) * 7 + (P(), P()),
        out_specs=(tokens, tokens) + (rows,) * 21 + (P(),) * 6,
        check_vma=False,
    )
```

```python
import functools
import math

import jax
import jax.numpy as jnp
import numpy as np
from jax import lax
from jax.experimental import pallas as pl
from jax.experimental.pallas import tpu as pltpu
from jax.sharding import PartitionSpec as P

QUERY_HEADS = 12
KEY_VALUE_HEADS = 2
HEAD_DIM = 128
CORES = 2
TILE = 256
VMEM_BYTES = 56 * 2**20

NORM_EPSILON = 1e-06
ROPE_BASE = 1000000.0
POLY_ONE = 3.4445
POLY_THREE = -4.775
POLY_FIVE = 2.0315
MOMENTUM = 0.95
STEP_SCALE = 0.06
VECTOR_STEP = 0.1
MASK_FILL = -1e30

F32 = jnp.float32
BF16 = jnp.bfloat16


def matmul(left, right):
    return jnp.dot(left, right, preferred_element_type=F32)


def matmul_nt(left, right):
    return lax.dot_general(left, right, (((1,), (1,)), ((), ())), preferred_element_type=F32)


def matmul_tn(left, right):
    return lax.dot_general(left, right, (((0,), (0,)), ((), ())), preferred_element_type=F32)


def after(value, *others):
    return lax.optimization_barrier((value,) + others)[0]


class Grid:
    def __init__(self, ctx_count, z_count):
        plane = ctx_count // CORES
        x_count = math.isqrt(plane)
        while plane % x_count:
            x_count -= 1
        self.x_count, self.y_count, self.z_count = x_count, plane // x_count, z_count

    def place(self):
        ctx = lax.axis_index("ctx")
        return (
            ctx // (CORES * self.x_count),
            (ctx // CORES) % self.x_count,
            ctx % CORES,
            lax.axis_index("fsdp"),
        )

    def shift(self, value, dy=0, dx=0, dc=0, dz=0, dpair=0, dhigh=0, keep=None):
        y_count, x_count, z_count = self.y_count, self.x_count, self.z_count
        if dz or dpair or dhigh:
            pairs = []
            for z in range(z_count):
                high, low = (z // 2 + dhigh) % (z_count // 2), (z % 2 + dpair) % 2
                pairs.append((z, (high * 2 + low + dz) % z_count))
            return lax.ppermute(value, "fsdp", pairs)
        dy, dx, dc = dy % y_count, dx % x_count, dc % CORES
        if not (dy or dx or dc):
            return value
        pairs = []
        for y in range(y_count):
            for x in range(x_count):
                for c in range(CORES):
                    to_y, to_x, to_c = (y + dy) % y_count, (x + dx) % x_count, (c + dc) % CORES
                    if keep is None or keep(to_y, to_x):
                        pairs.append(
                            ((y * x_count + x) * CORES + c, (to_y * x_count + to_x) * CORES + to_c)
                        )
        return lax.ppermute(value, "ctx", pairs)

    def gather_first(self, block):
        half = block.shape[0] // 2
        first, second = block[:half], block[half:]
        return (
            [first] + [self.shift(first, dx=j) for j in range(1, self.x_count)],
            [second] + [self.shift(second, dy=j) for j in range(1, self.y_count)],
        )

    def plane_gather(self, block, *others):
        halves = self.gather_first(block)
        return self.gather_second(*(after(halves, *others) if others else halves))

    def gather_second(self, first, second):
        first, second = jnp.concatenate(first), jnp.concatenate(second)
        return jnp.concatenate(
            [first]
            + [self.shift(first, dy=j) for j in range(1, self.y_count)]
            + [second]
            + [self.shift(second, dx=j) for j in range(1, self.x_count)]
        )

    def plane_order(self, rows):
        half = rows // 2
        jy, jx, row = [], [], []
        for y in range(self.y_count):
            for x in range(self.x_count):
                for r in range(half):
                    jy.append(y), jx.append(x), row.append(r)
        for x in range(self.x_count):
            for y in range(self.y_count):
                for r in range(half, rows):
                    jy.append(y), jx.append(x), row.append(r)
        return np.array(jy), np.array(jx), np.array(row)

    def z_slots(self, block, ring=False):
        if ring:
            slots = [block]
            for _ in range(1, self.z_count):
                slots.append(self.shift(slots[-1], dz=1))
            return slots
        return [block] + [self.shift(block, dz=j) for j in range(1, self.z_count)]

    def gather(self, slots):
        size = self.z_count // 2
        return [
            self.plane_gather(jnp.concatenate(slots[k : k + size]))
            for k in range(0, self.z_count, size)
        ]

    def gather_order(self, rows):
        size = self.z_count // 2
        jy, jx, row = self.plane_order(size * rows)
        jz = [k + row // rows for k in range(0, self.z_count, size)]
        return jz, jy, jx, row % rows

    def step(self, rows, count, axis):
        size = rows.shape[0] // count
        total = rows[:size].astype(F32)
        for j in range(1, count):
            piece = rows[j * size : (j + 1) * size].astype(BF16)
            total = total + self.shift(piece, **{axis: -j}).astype(F32)
        return total

    def reduce_first(self, part):
        half = part.shape[0] // 2
        return (
            self.step(part[:half], self.y_count, "dy"),
            self.step(part[half:], self.x_count, "dx"),
        )

    def reduce_second(self, first, second):
        return jnp.concatenate(
            [self.step(first, self.x_count, "dx"), self.step(second, self.y_count, "dy")]
        )

    def plane_reduce(self, part):
        return self.reduce_second(*self.reduce_first(part))

    def z_sum(self, parts):
        total = parts[0].astype(F32)
        for j in range(1, self.z_count):
            total = total + self.shift(parts[j].astype(BF16), dz=-j).astype(F32)
        return total

    def by_slot(self, totals):
        slots = []
        for total in totals:
            size = self.z_count // len(totals)
            rows = total.shape[0] // size
            slots += [total[k * rows : (k + 1) * rows] for k in range(size)]
        return slots

    def token_gather(self, block, *others):
        slots = [block] + [
            self.shift(block, dhigh=j) for j in range(1, self.z_count // 2)
        ]
        if others:
            slots[1:] = after(slots[1:], *others)
        return [self.plane_gather(slots[0], *others)] + [
            self.plane_gather(slot) for slot in slots[1:]
        ]

    def token_reduce(self, halves):
        sums = [self.reduce_second(*half) for half in halves]
        return sums[:1] + [
            self.shift(sums[j].astype(BF16), dhigh=-j) for j in range(1, len(sums))
        ]

    def total(self, value):
        for axis, count in (("ctx", self.y_count * self.x_count * CORES), ("fsdp", self.z_count)):
            step = 1
            while step < count:
                value = value + lax.ppermute(value, axis, [(k, k ^ step) for k in range(count)])
                step *= 2
        return value


def rope_tables(positions, head_size):
    half_width = head_size // 2
    ratios = jnp.arange(half_width, dtype=F32) * (2.0 / head_size)
    frequency = jnp.exp(-math.log(ROPE_BASE) * ratios)
    angles = positions.astype(F32)[:, None] * frequency[None, :]
    cosine, sine = jnp.cos(angles), jnp.sin(angles)
    return jnp.concatenate([cosine, cosine], axis=1), jnp.concatenate([-sine, sine], axis=1)


def norm_scale(values):
    return lax.rsqrt(jnp.mean(values * values, axis=-1, keepdims=True) + NORM_EPSILON)


def norm_back(values, scale_rows, gain, grad_normed):
    weighted = grad_normed * gain
    inner_mean = jnp.mean(weighted * values, axis=-1, keepdims=True)
    grad_values = (
        scale_rows * weighted - values * (scale_rows * scale_rows * scale_rows) * inner_mean
    )
    grad_gain = jnp.sum(grad_normed * values * scale_rows, axis=0, keepdims=True)
    return (grad_values, grad_gain)


def rotate(head, cosine, sine):
    return head * cosine + pltpu.roll(head, HEAD_DIM // 2, 1) * sine


def head_columns(head):
    return slice(head * HEAD_DIM, (head + 1) * HEAD_DIM)


def by_pieces(rows, piece_refs):
    total, start = 0.0, 0
    for ref in piece_refs:
        size = ref.shape[0]
        total = total + matmul(rows[:, start : start + size], ref[...])
        start += size
    return total


def by_pieces_nt(rows, piece_refs):
    return jnp.concatenate([matmul_nt(rows, ref[...]) for ref in piece_refs], axis=1)


def compute(kernel, outs, args, flops, scratch=()):
    return pl.pallas_call(
        kernel,
        out_shape=[jax.ShapeDtypeStruct(shape, dtype) for shape, dtype in outs],
        scratch_shapes=scratch,
        compiler_params=pltpu.CompilerParams(vmem_limit_bytes=VMEM_BYTES),
        cost_estimate=pl.CostEstimate(flops=flops, bytes_accessed=2**20, transcendentals=0),
    )(*args)


def project_kernel(
    tokens_ref, gains_ref, bias_ref, cosine_ref, sine_ref, reorder_ref, *refs
):
    piece_refs, (normed_ref, query_ref, key_value_ref) = refs[:-3], refs[-3:]
    inputs = tokens_ref[...].astype(F32)
    normed = (inputs * norm_scale(inputs) * gains_ref[0:1, :].astype(F32)).astype(BF16)
    normed = matmul(normed, reorder_ref[...]).astype(BF16)
    normed_ref[...] = normed
    projected = by_pieces(normed, piece_refs) + bias_ref[...].astype(F32)
    cosine, sine = cosine_ref[...], sine_ref[...]
    for head in range(QUERY_HEADS):
        rotated = rotate(projected[:, head_columns(head)], cosine, sine)
        query_ref[:, head_columns(head)] = rotated.astype(BF16)
    for head in range(2 * KEY_VALUE_HEADS):
        values = projected[:, head_columns(QUERY_HEADS + head)]
        if head < KEY_VALUE_HEADS:
            values = rotate(values, cosine, sine)
        key_value_ref[:, head_columns(head)] = values.astype(BF16)


def attend_kernel(piece_count, tokens_ref, gains_ref, reorder_ref, query_ref, rows_ref, keys_ref, *refs):
    key_value_refs, refs = refs[:piece_count], refs[piece_count:]
    weight_refs, refs = refs[:-6], refs[-6:]
    mixed_ref, log_ref, attended_ref, hidden_ref, normed_ref, all_ref = refs
    size = key_value_refs[0].shape[0]
    for k, ref in enumerate(key_value_refs):
        all_ref[k * size : (k + 1) * size, :] = ref[...]
    visible = keys_ref[...] <= rows_ref[...]
    scale = 1.0 / math.sqrt(HEAD_DIM)
    group = QUERY_HEADS // KEY_VALUE_HEADS
    attended = []
    log_ref[...] = jnp.zeros(log_ref.shape, F32)
    for head in range(QUERY_HEADS):
        keys = all_ref[:, head_columns(head // group)]
        values = all_ref[:, head_columns(KEY_VALUE_HEADS + head // group)]
        scores = matmul_nt(query_ref[:, head_columns(head)], keys) * scale
        scores = jnp.where(visible, scores, MASK_FILL)
        peak = jnp.max(scores, axis=-1, keepdims=True)
        weights = jnp.exp(scores - peak)
        total = jnp.sum(weights, axis=-1, keepdims=True)
        log_ref[:, head : head + 1] = peak + jnp.log(total)
        mixed = matmul((weights * (1.0 / total)).astype(BF16), values)
        mixed_ref[:, head_columns(head)] = mixed
        attended.append(mixed.astype(BF16))
    attended = jnp.concatenate(attended, axis=1)
    attended = matmul(attended, reorder_ref[...]).astype(BF16)
    attended_ref[...] = attended
    hidden = tokens_ref[...].astype(F32) + by_pieces(attended, weight_refs)
    hidden_ref[...] = hidden
    normed_ref[...] = (hidden * norm_scale(hidden) * gains_ref[1:2, :].astype(F32)).astype(BF16)


def attend_back_kernel(
    piece_count,
    grad_count,
    cotangent_ref,
    gains_ref,
    hidden_ref,
    reorder_ref,
    query_ref,
    rows_ref,
    keys_ref,
    cosine_ref,
    sine_ref,
    mixed_ref,
    log_ref,
    *refs,
):
    grad_refs, refs = refs[:grad_count], refs[grad_count:]
    key_value_refs, refs = refs[:piece_count], refs[piece_count:]
    outs = 4 + piece_count
    weight_refs, refs = refs[: -outs - 3], refs[-outs - 3 :]
    hidden_grad_ref, branch_ref, gain_ref, query_grad_ref = refs[:4]
    piece_refs, (all_ref, key_sum, value_sum) = refs[4:outs], refs[outs:]
    size = key_value_refs[0].shape[0]
    for k, ref in enumerate(key_value_refs):
        all_ref[k * size : (k + 1) * size, :] = ref[...]
    hidden = hidden_ref[...]
    grad_normed = sum(ref[...].astype(F32) for ref in grad_refs)
    grad, grad_gain = norm_back(
        hidden, norm_scale(hidden), gains_ref[1:2, :].astype(F32), grad_normed
    )
    gain_ref[...] = grad_gain
    grad = grad + cotangent_ref[...].astype(F32)
    hidden_grad_ref[...] = grad
    branch = grad.astype(BF16)
    branch_ref[...] = branch
    attended_grad = by_pieces_nt(branch, weight_refs).astype(BF16)
    attended_grad = matmul_nt(attended_grad, reorder_ref[...]).astype(BF16)
    visible = keys_ref[...] <= rows_ref[...]
    scale = 1.0 / math.sqrt(HEAD_DIM)
    group = QUERY_HEADS // KEY_VALUE_HEADS
    cosine, sine = cosine_ref[...], sine_ref[...]
    for head in range(QUERY_HEADS):
        kind = head // group
        keys = all_ref[:, head_columns(kind)]
        values = all_ref[:, head_columns(KEY_VALUE_HEADS + kind)]
        query = query_ref[:, head_columns(head)]
        own = attended_grad[:, head_columns(head)]
        scores = matmul_nt(query, keys) * scale
        soft = jnp.exp(jnp.where(visible, scores, MASK_FILL) - log_ref[:, head : head + 1])
        inner = jnp.sum(
            own.astype(F32) * mixed_ref[:, head_columns(head)], axis=-1, keepdims=True
        )
        score_grad = (soft * (matmul_nt(own, values) - inner)).astype(BF16)
        query_grad = matmul(score_grad, keys) * scale
        query_grad_ref[:, head_columns(head)] = rotate(query_grad, cosine, -sine).astype(BF16)
        key_part = matmul_tn(score_grad, query)
        value_part = matmul_tn(soft.astype(BF16), own)
        if head % group == 0:
            key_sum[...] = key_part
            value_sum[...] = value_part
        else:
            key_sum[...] += key_part
            value_sum[...] += value_part
        if head % group == group - 1:
            for k, ref in enumerate(piece_refs):
                rows = slice(k * size, (k + 1) * size)
                ref[:, head_columns(kind)] = (key_sum[rows, :] * scale).astype(BF16)
                ref[:, head_columns(KEY_VALUE_HEADS + kind)] = value_sum[rows, :].astype(BF16)


def weights_back_kernel(
    tokens_ref,
    gains_ref,
    reorder_ref,
    cosine_ref,
    sine_ref,
    normed_ref,
    attended_ref,
    branch_ref,
    hidden_grad_ref,
    query_grad_ref,
    pair_ref,
    other_ref,
    *refs,
):
    weight_refs, refs = refs[:-6], refs[-6:]
    own_ref, sent_ref, tokens_grad_ref, bias_ref, gain_ref, grad_ref = refs
    query_width = query_grad_ref.shape[1]
    grad_ref[:, :query_width] = query_grad_ref[...]
    key_value = pair_ref[...] + other_ref[...].astype(F32)
    cosine, sine = cosine_ref[...], sine_ref[...]
    for head in range(2 * KEY_VALUE_HEADS):
        values = key_value[:, head_columns(head)]
        if head < KEY_VALUE_HEADS:
            values = rotate(values, cosine, -sine)
        grad_ref[:, head_columns(QUERY_HEADS + head)] = values.astype(BF16)
    grad = grad_ref[...]
    bias_ref[...] = jnp.sum(grad.astype(F32), axis=0, keepdims=True)
    qkv_width = grad.shape[1]
    branch = branch_ref[...]
    size = own_ref.shape[1]
    for k in range(2 * CORES):
        out = sent_ref if k % CORES else own_ref
        rows = slice(k * size, (k + 1) * size)
        out[k // CORES, :, :qkv_width] = matmul_tn(normed_ref[:, rows], grad).astype(BF16)
        out[k // CORES, :, qkv_width:] = matmul_tn(attended_ref[:, rows], branch).astype(BF16)
    normed_grad = by_pieces_nt(grad, weight_refs)
    high = normed_grad.astype(BF16)
    low = (normed_grad - high.astype(F32)).astype(BF16)
    reorder = reorder_ref[...]
    normed_grad = matmul_nt(high, reorder) + matmul_nt(low, reorder)
    inputs = tokens_ref[...].astype(F32)
    grad, grad_gain = norm_back(
        inputs, norm_scale(inputs), gains_ref[0:1, :].astype(F32), normed_grad
    )
    gain_ref[...] = grad_gain
    tokens_grad_ref[...] = grad + hidden_grad_ref[...]


def vector_step(old_state, gradient):
    fresh_state = MOMENTUM * old_state + gradient
    inverse_rms = lax.rsqrt(
        jnp.mean(fresh_state * fresh_state, axis=-1, keepdims=True) + NORM_EPSILON
    )
    return (fresh_state, -VECTOR_STEP * fresh_state * inverse_rms)


def packed_height(width):
    count = width // TILE
    return count * (count + 1) // 2 * TILE


def packed_block(row, column, count):
    return pl.ds((row * count - row * (row - 1) // 2 + column - row) * TILE, TILE)


def block_rows(index):
    return slice(index * TILE, (index + 1) * TILE)


def gram_kernel(start_ref, packed_ref):
    count = start_ref.shape[1] // TILE
    for i in range(count):
        row = lax.dot_general(
            start_ref[:, block_rows(i)],
            start_ref[:, i * TILE :],
            (((0,), (0,)), ((), ())),
            preferred_element_type=F32,
        )
        for j in range(i, count):
            packed_ref[packed_block(i, j, count), :] = row[:, block_rows(j - i)].astype(
                packed_ref.dtype
            )


def gram_packed(start, dtype):
    rows, width = start.shape
    height = packed_height(width)
    return pl.pallas_call(
        gram_kernel,
        out_shape=jax.ShapeDtypeStruct((height, TILE), dtype),
        compiler_params=pltpu.CompilerParams(vmem_limit_bytes=VMEM_BYTES),
        cost_estimate=pl.CostEstimate(
            flops=rows * width * width,
            bytes_accessed=2 * rows * width + 4 * height * TILE,
            transcendentals=0,
        ),
    )(start)


def chain_kernel(packed_ref, start_ref, new_ref, low, poly, mixed, two):
    count = start_ref.shape[1] // TILE

    def put(ref, i, j, block):
        ref[block_rows(i), block_rows(j)] = block
        if i != j:
            ref[block_rows(j), block_rows(i)] = block.T

    def product(left, right):
        for i in range(count):
            row = jnp.dot(left[block_rows(i), :], right[:, i * TILE :], preferred_element_type=F32)
            for j in range(i, count):
                yield i, j, row[:, block_rows(j - i)]

    same = lax.broadcasted_iota(jnp.int32, (TILE, TILE), 0) == lax.broadcasted_iota(
        jnp.int32, (TILE, TILE), 1
    )
    trace = jnp.zeros((1, 1), F32)
    for i in range(count):
        block = packed_ref[packed_block(i, i, count), :].astype(F32)
        trace = trace + jnp.sum(jnp.where(same, block, 0.0), keepdims=True)
    factor = 1.0 / (jnp.sqrt(trace) + 1e-07)
    square = factor * factor

    def gram_one(i, j):
        return packed_ref[packed_block(i, j, count), :].astype(F32) * square

    for i in range(count):
        for j in range(i, count):
            put(low, i, j, gram_one(i, j).astype(BF16))
    for i, j, block in product(low, low):
        put(poly, i, j, (POLY_THREE * gram_one(i, j) + POLY_FIVE * block).astype(BF16))
    for i, j, block in product(low, poly):
        two[packed_block(i, j, count), :] = (POLY_ONE * POLY_ONE) * gram_one(i, j) + (
            2.0 * POLY_ONE
        ) * block
        put(mixed, i, j, block.astype(BF16))
    for i, j, block in product(poly, mixed):
        block = two[packed_block(i, j, count), :] + block
        two[packed_block(i, j, count), :] = block
        put(low, i, j, block.astype(BF16))
    start = start_ref[...]
    middle = jnp.dot(start, poly[...], preferred_element_type=F32)
    middle = (factor * (POLY_ONE * start.astype(F32) + middle)).astype(BF16)
    for i, j, block in product(low, low):
        block = POLY_THREE * two[packed_block(i, j, count), :] + POLY_FIVE * block
        put(mixed, i, j, block.astype(BF16))
    new = jnp.dot(middle, mixed[...], preferred_element_type=F32)
    new_ref[...] = (POLY_ONE * middle.astype(F32) + new).astype(BF16)


def orthogonalize(packed, start):
    rows, width = start.shape
    return pl.pallas_call(
        chain_kernel,
        out_shape=jax.ShapeDtypeStruct(start.shape, BF16),
        scratch_shapes=[
            pltpu.VMEM((width, width), BF16),
            pltpu.VMEM((width, width), BF16),
            pltpu.VMEM((width, width), BF16),
            pltpu.VMEM((packed_height(width), TILE), F32),
        ],
        compiler_params=pltpu.CompilerParams(vmem_limit_bytes=VMEM_BYTES),
        cost_estimate=pl.CostEstimate(
            flops=5 * width**3 + 4 * rows * width * width,
            bytes_accessed=4 * rows * width + 4 * packed_height(width) * TILE,
            transcendentals=0,
        ),
    )(packed, start)


def shards(
    tokens,
    cotangent,
    block_position,
    w_query,
    key_weight,
    value_weight,
    w_output,
    w_gate,
    w_up,
    w_down,
    projection_bias,
    norm_gains,
    momentum_query,
    key_momentum,
    value_momentum,
    momentum_output,
    momentum_gate,
    momentum_up,
    momentum_down,
    bias_momentum,
    momentum_gains,
):
    shard_rows = tokens.shape[1]
    width = tokens.shape[2]
    ctx_count = lax.axis_size("ctx")
    z_count = lax.axis_size("fsdp")
    grid = Grid(ctx_count, z_count)
    y_count, x_count = grid.y_count, grid.x_count
    plane = y_count * x_count
    place_y, place_x, place_c, place_z = grid.place()
    ctx_rank = lax.axis_index("ctx")
    all_count = ctx_count * z_count
    half_block = shard_rows // 2
    query_width = QUERY_HEADS * HEAD_DIM
    key_value_width = KEY_VALUE_HEADS * HEAD_DIM
    weight_rows = w_query.shape[0]
    ff_rows = w_gate.shape[0]

    def both_cores(chunks):
        parts = []
        for chunk in chunks:
            parts += [chunk, grid.shift(chunk, dc=1)]
        return parts

    qkv_width = query_width + 2 * key_value_width
    qkv_slots = grid.z_slots(jnp.concatenate([w_query, key_weight, value_weight], axis=1))
    qkv_chunks = grid.gather(qkv_slots)
    qkv_pieces = both_cores(qkv_chunks)
    output_slots = grid.z_slots(after(w_output, qkv_slots[-1]))
    output_first = output_slots[-1]
    output_slots = after(output_slots, *qkv_chunks)
    size = z_count // 2
    output_halves = [
        grid.gather_first(jnp.concatenate(output_slots[k : k + size])) for k in range(0, z_count, size)
    ]
    tokens = after(tokens, qkv_slots[-1])
    place_y, place_x, place_c, place_z = after(
        (place_y, place_x, place_c, place_z), qkv_slots[-1]
    )
    jz_parts, jy, jx, row = grid.gather_order(weight_rows)
    source_y = (place_y - jnp.asarray(jy)) % y_count
    source_x = (place_x - jnp.asarray(jx)) % x_count
    pieces = []
    for jz in jz_parts:
        source_z = (place_z - jnp.asarray(jz)) % z_count
        for jc in range(CORES):
            source_ctx = (source_y * x_count + source_x) * CORES + (place_c - jc) % CORES
            pieces.append((source_ctx * z_count + source_z) * weight_rows + jnp.asarray(row))
    relative_rows = jnp.concatenate(pieces)
    reorder = (jnp.arange(width, dtype=jnp.int32)[:, None] == relative_rows[None, :]).astype(BF16)

    own_tokens = tokens[0]
    grad_mid = cotangent[0]

    shared = 2 * CORES
    ff_weights = after((w_gate, w_up, w_down), qkv_slots[-1], output_first)
    ff_pairs = [grid.shift(weight, dpair=1) for weight in ff_weights]

    own_positions = (
        lax.dynamic_slice_in_dim(block_position, 2 * ctx_rank, 2)[:, None] * half_block
        + jnp.arange(half_block, dtype=jnp.int32)[None, :]
    ).reshape(shard_rows)
    cosine_lookup, sine_lookup = rope_tables(own_positions, HEAD_DIM)
    row_positions = own_positions[:, None]
    normed_relative, queries, key_value = compute(
        project_kernel,
        [
            ((shard_rows, width), BF16),
            ((shard_rows, query_width), BF16),
            ((shard_rows, 2 * key_value_width), BF16),
        ],
        [
            after(after(own_tokens, output_halves), ff_pairs[0]),
            norm_gains,
            projection_bias[None, :],
            cosine_lookup,
            sine_lookup,
            reorder,
            *qkv_pieces,
        ],
        2 * shard_rows * width * qkv_width,
    )
    key_value_pair = jnp.concatenate([key_value, grid.shift(key_value, dc=1)])
    places = [(jy_, jx_) for jy_ in range(y_count) for jx_ in range(x_count)]
    key_value_pieces = [grid.shift(key_value_pair, dy=a, dx=b) for a, b in places]
    output_chunks = [grid.gather_second(*half) for half in output_halves]
    output_pieces = both_cores(output_chunks)
    ff_chips = [jnp.concatenate(pair) for pair in zip(ff_weights, ff_pairs)]
    ff_others = [grid.shift(chip, dc=1) for chip in ff_chips]
    gate_shared, up_shared, down_shared = (
        jnp.concatenate(pair) for pair in zip(ff_chips, ff_others)
    )
    key_ctx = jnp.stack(
        [
            (((place_y - a) % y_count) * x_count + (place_x - b) % x_count) * CORES
            + (place_c - j) % CORES
            for a, b in places
            for j in range(CORES)
        ]
    )
    key_positions = (
        jnp.take(block_position.reshape(ctx_count, 2), key_ctx, axis=0)[:, :, None] * half_block
        + jnp.arange(half_block, dtype=jnp.int32)[None, None, :]
    ).reshape(1, shard_rows * ctx_count)
    seq_length = shard_rows * ctx_count

    mixed, log_total, attended_relative, hidden_one, normed_two = compute(
        functools.partial(attend_kernel, plane),
        [
            ((shard_rows, query_width), F32),
            ((shard_rows, HEAD_DIM), F32),
            ((shard_rows, query_width), BF16),
            ((shard_rows, width), F32),
            ((shard_rows, width), BF16),
        ],
        [
            after(own_tokens, gate_shared, up_shared, down_shared),
            norm_gains,
            reorder,
            queries,
            row_positions,
            key_positions,
            *key_value_pieces,
            *output_pieces,
        ],
        4 * shard_rows * width * width,
        [pltpu.VMEM((seq_length, 2 * key_value_width), BF16)],
    )

    grad_chunks = grid.token_gather(
        after(grad_mid, *key_value_pieces, output_chunks[-1]), normed_two
    )

    normed_chunks = grid.token_gather(normed_two)
    out_parts, normed_grad_parts = [], []
    gate_sum = up_sum = down_sum = 0.0
    for normed_chunk, grad_chunk in zip(normed_chunks, grad_chunks):
        gate_values = matmul_nt(normed_chunk, gate_shared)
        up_values = matmul_nt(normed_chunk, up_shared)
        grad_hidden = matmul_nt(grad_chunk, down_shared)
        sigmoid_gate = jax.nn.sigmoid(gate_values)
        active = gate_values * sigmoid_gate
        hidden = (active * up_values).astype(BF16)
        up_low = (grad_hidden * active).astype(BF16)
        gate_low = (
            grad_hidden * up_values * (sigmoid_gate * (1.0 + gate_values * (1.0 - sigmoid_gate)))
        ).astype(BF16)
        normed_grad_parts.append(
            (matmul(gate_low, gate_shared) + matmul(up_low, up_shared)).astype(BF16)
        )
        gate_sum = gate_sum + matmul_tn(gate_low, normed_chunk)
        up_sum = up_sum + matmul_tn(up_low, normed_chunk)
        down_sum = down_sum + matmul_tn(hidden, grad_chunk)
        out_parts.append(matmul(hidden, down_shared).astype(BF16))

    def chip_rows(total):
        other = grid.shift(total[2 * ff_rows :].astype(BF16), dc=1)
        return total[: 2 * ff_rows] + other.astype(F32)

    def own_rows(chip_sum):
        piece = grid.shift(chip_sum[ff_rows:].astype(BF16), dpair=1)
        return chip_sum[:ff_rows] + piece.astype(F32)

    chip_sums = [chip_rows(total) for total in (gate_sum, up_sum, down_sum)]
    grad_gate, grad_up, grad_down = [own_rows(chip_sum) for chip_sum in chip_sums]
    moment_gate = MOMENTUM * momentum_gate + grad_gate
    moment_up = MOMENTUM * momentum_up + grad_up
    moment_down = MOMENTUM * momentum_down + grad_down

    ff_start = jnp.stack([m.astype(BF16) for m in (moment_gate, moment_up, moment_down)])

    ff_count = ff_start.shape[0]

    def weight_at(a, b):
        column = ((place_y + a) % y_count) * x_count + (place_x + b) % x_count
        return lax.dynamic_index_in_dim(
            ff_start, jnp.minimum(column, ff_count - 1), axis=0, keepdims=False
        )

    def has_weight(y, x):
        return y * x_count + x < ff_count

    shipped = [
        grid.shift(weight_at(a, b), dy=a, dx=b, keep=has_weight) for a, b in places
    ]

    normed_grad_sums = grid.token_reduce([grid.reduce_first(part) for part in normed_grad_parts])
    hidden_grad, grad_branch, grad_gain_two, query_grad, *key_value_grads = compute(
        functools.partial(attend_back_kernel, plane, len(normed_grad_sums)),
        [
            ((shard_rows, width), F32),
            ((shard_rows, width), BF16),
            ((1, width), F32),
            ((shard_rows, query_width), BF16),
        ]
        + [((CORES * shard_rows, 2 * key_value_width), BF16)] * plane,
        [
            grad_mid,
            norm_gains,
            after(hidden_one, *chip_sums),
            reorder,
            queries,
            row_positions,
            key_positions,
            cosine_lookup,
            sine_lookup,
            mixed,
            log_total,
            *normed_grad_sums,
            *key_value_pieces,
            *output_pieces,
        ],
        4 * shard_rows * width * width,
        [
            pltpu.VMEM((seq_length, 2 * key_value_width), BF16),
            pltpu.VMEM((seq_length, HEAD_DIM), F32),
            pltpu.VMEM((seq_length, HEAD_DIM), F32),
        ],
    )
    key_value_grads = after(key_value_grads, grad_gate)
    pair_grad = sum(
        grid.shift(piece, dy=-a, dx=-b).astype(F32)
        for piece, (a, b) in zip(key_value_grads, places)
    )
    key_value_other = grid.shift(pair_grad[shard_rows:].astype(BF16), dc=1)

    weight_shape = (2, weight_rows * all_count // (2 * CORES), qkv_width + width)
    weight_own, weight_sent, grad_tokens, bias_term, grad_gain_one = compute(
        weights_back_kernel,
        [
            (weight_shape, BF16),
            (weight_shape, BF16),
            ((shard_rows, width), F32),
            ((1, qkv_width), F32),
            ((1, width), F32),
        ],
        [
            own_tokens,
            norm_gains,
            reorder,
            cosine_lookup,
            sine_lookup,
            normed_relative,
            attended_relative,
            grad_branch,
            hidden_grad,
            query_grad,
            pair_grad[:shard_rows],
            key_value_other,
            *qkv_pieces,
        ],
        4 * shard_rows * width * qkv_width,
        [pltpu.VMEM((shard_rows, qkv_width), BF16)],
    )
    other = grid.shift(weight_sent, dc=1)
    other = after(other, ff_start)
    weight_sum = (weight_own.astype(F32) + other.astype(F32)).astype(BF16)
    attention_halves = [grid.reduce_first(weight_sum[j]) for j in range(2)]
    attention_slots = grid.by_slot([grid.reduce_second(*halves) for halves in attention_halves])
    attention_grads = grid.z_sum(attention_slots)
    grad_query = attention_grads[:, :query_width]
    grad_key = attention_grads[:, query_width : query_width + key_value_width]
    grad_value = attention_grads[:, query_width + key_value_width : qkv_width]
    grad_output = attention_grads[:, qkv_width:]

    moment_query = MOMENTUM * momentum_query + grad_query
    moment_key = MOMENTUM * key_momentum + grad_key
    moment_value = MOMENTUM * value_momentum + grad_value
    moment_output = MOMENTUM * momentum_output + grad_output
    query_key = jnp.concatenate([moment_query, moment_key], axis=1).astype(BF16)
    output_value = jnp.concatenate([moment_output, moment_value], axis=1).astype(BF16)
    mine = jnp.where(place_c == 0, query_key, output_value)
    theirs = jnp.where(place_c == 0, output_value, query_key)
    pair_start = jnp.concatenate([mine, grid.shift(theirs, dc=1)])
    start_slots = grid.z_slots(pair_start, ring=True)
    start_all = jnp.concatenate(grid.gather(start_slots))

    current = jnp.concatenate(shipped)
    gram_part = gram_packed(current, BF16)
    half_rows = gram_part.shape[0] // CORES
    kept = lax.dynamic_slice_in_dim(gram_part, place_c * half_rows, half_rows)
    sent = lax.dynamic_slice_in_dim(gram_part, (1 - place_c) * half_rows, half_rows)
    gram_half = (kept.astype(F32) + grid.shift(sent, dc=1).astype(F32)).astype(BF16)
    gram_half = after(gram_half, weight_sum)
    z_rows = half_rows // z_count
    gram_own = grid.z_sum(
        [
            lax.dynamic_slice_in_dim(gram_half, ((place_z - j) % z_count) * z_rows, z_rows)
            for j in range(z_count)
        ]
    ).astype(BF16)
    gram_own = after(gram_own, *attention_halves)
    gram_half = jnp.zeros((half_rows, TILE), BF16)
    for j, piece in enumerate(grid.z_slots(gram_own, ring=True)):
        gram_half = lax.dynamic_update_slice_in_dim(
            gram_half, piece, ((place_z - j) % z_count) * z_rows, axis=0
        )
    gram_half = after(gram_half, *attention_slots)
    gram_other = grid.shift(gram_half, dc=1)
    gram = jnp.where(
        place_c == 0,
        jnp.concatenate([gram_half, gram_other]),
        jnp.concatenate([gram_other, gram_half]),
    )
    moved = orthogonalize(after(gram, *start_slots), current)
    back_pieces = [
        grid.shift(moved[k * ff_rows : (k + 1) * ff_rows], dy=-a, dx=-b)
        for k, (a, b) in enumerate(places)
    ]
    back = jnp.stack(back_pieces)

    def ff_update(index):
        a = (index // x_count - place_y) % y_count
        b = (index % x_count - place_x) % x_count
        rows = lax.dynamic_index_in_dim(back, a * x_count + b, axis=0, keepdims=False)
        scale = -STEP_SCALE * math.sqrt(max(ff_rows * all_count, width))
        return scale * rows.astype(F32)

    update_gate, update_up, update_down = ff_update(0), ff_update(1), ff_update(2)

    start_all = after(start_all, moved)
    large, small = start_all[:, :width], start_all[:, width:]
    large_new = orthogonalize(gram_packed(large, F32), pair_start[:, :width])
    small_new = orthogonalize(gram_packed(small, F32), pair_start[:, width:])
    pair_new = jnp.concatenate([large_new, small_new], axis=1)
    mine_new = pair_new[:weight_rows]
    theirs_new = grid.shift(pair_new[weight_rows:], dc=1)
    query_key_new = jnp.where(place_c == 0, mine_new, theirs_new).astype(F32)
    output_value_new = jnp.where(place_c == 0, theirs_new, mine_new).astype(F32)
    scale = -STEP_SCALE * math.sqrt(max(weight_rows * all_count, width))
    kv_scale = -STEP_SCALE * math.sqrt(max(weight_rows * all_count, key_value_width))
    update_query = scale * query_key_new[:, :width]
    update_key = kv_scale * query_key_new[:, width:]
    update_output = scale * output_value_new[:, :width]
    update_value = kv_scale * output_value_new[:, width:]

    vectors = grid.total(
        jnp.concatenate([bias_term, grad_gain_one, grad_gain_two], axis=1).reshape(-1, HEAD_DIM)
    ).reshape(-1)
    grad_bias = vectors[:qkv_width]
    grad_gains = vectors[qkv_width:].reshape(2, width)
    moment_bias, update_bias = vector_step(bias_momentum, grad_bias)
    moment_gains, update_gains = vector_step(momentum_gains, grad_gains)

    out_terms = grid.token_reduce(
        [grid.reduce_first(after(part, gram_own)) for part in out_parts]
    )
    out_terms[1:] = after(out_terms[1:], moved)
    out_tokens = sum((term.astype(F32) for term in out_terms), hidden_one).astype(BF16)[None]
    return (
        out_tokens,
        grad_tokens[None],
        grad_query,
        grad_key,
        grad_value,
        grad_output,
        grad_gate,
        grad_up,
        grad_down,
        moment_query,
        moment_key,
        moment_value,
        moment_output,
        moment_gate,
        moment_up,
        moment_down,
        update_query,
        update_key,
        update_value,
        update_output,
        update_gate,
        update_up,
        update_down,
        grad_bias,
        moment_bias,
        update_bias,
        grad_gains,
        moment_gains,
        update_gains,
    )


def solution(mesh):
    tokens = P("fsdp", "ctx", None)
    rows = P(("ctx", "fsdp"), None)
    return jax.shard_map(
        shards,
        mesh=mesh,
        in_specs=(tokens, tokens, P()) + (rows,) * 7 + (P(), P()) + (rows,) * 7 + (P(), P()),
        out_specs=(tokens, tokens) + (rows,) * 21 + (P(),) * 6,
        check_vma=False,
    )
```
